32 devices in a mesh: dir: 4 (over x, core), space: 8 (over z, y).
Axes of the slice: x: 2, y: 2, z: 4, core: 2. Of those that a mesh axis runs over, the one named last changes fastest.
Arguments:
- store: float32 [4, 2, 32, 512, 128], P('dir', None, 'space'), may hold values from 0.2 to 1.5
- rate: float32 [32, 512, 128], P('space'), may hold values from 0.3 to 3
- directions: float32 [8, 8, 8192], P('dir', 'space'), may hold values from -6 to 6
- owner_map: int32 [4], replicated, may hold values from 0 to 3, each once
- block_map: int32 [8], replicated, may hold values from 0 to 7, each once
Outputs:
- tangent: float32 [8, 2, 32, 512, 128], P('dir', None, 'space')
- sens: float32 [8, 8, 8192], P('dir', 'space')
The draws below stay inside these ranges and needn't reach their ends.
All inputs are finite; a program needn't handle non-finite values.
Results may differ from the reference program's by a relative error of at most 0.000071.
Values sent between devices are 32-bit elements; how exact they have to be, the bound alone decides.
No kernel may reach another device: no remote copies, remote signals or barrier semaphores. Data moves between devices by JAX's collectives and lax.ppermute only.
A program may use at most 192 MiB of HBM per device.

```python
import math
import jax
import jax.numpy as jnp
from jax import lax

NY = 512
NZ = 128
STEPS = 2
SUBSTEPS = 3
DIRS = 8
NX = 32
CBLOCK = 8192
N_DIR = 4
N_SPACE = 8


def steps_of(rng, extent, split, least, high):
    loudness, own = 1.0, jax.random.fold_in(rng, 6)
    for axis_at, shards_of in split:
        heights = jnp.exp(jax.random.uniform(jax.random.fold_in(own, axis_at), (shards_of,), jnp.float32, least / len(split), high / len(split)))
        loudness = loudness * jnp.repeat(heights, extent[axis_at] // shards_of).reshape([-1 if axis == axis_at else 1 for axis in range(len(extent))])
    return loudness


def gaussian(key, dims, deviation, bound, shards=(), dtype=jnp.bfloat16):
    gain = steps_of(key, dims, shards, -0.22, 0.18) if shards else 1.0
    drawn = jax.random.normal(key, dims, jnp.float32) * deviation * gain
    return jnp.minimum(jnp.maximum(drawn, -bound), bound).astype(dtype)


def setup_inputs(seed: int = 0) -> dict:
    streams_of = jax.random.split(jax.random.key(seed), 6)
    store = jnp.clip(0.2 + 1.3 * jax.random.uniform(streams_of[0], (N_DIR, 2, NX, NY, NZ), jnp.float32) ** steps_of(streams_of[0], (N_DIR, 2, NX, NY, NZ), ((0, 4), (2, 8)), -0.2, 0.2), 0.2, 1.5)
    rate = jnp.clip(jnp.exp(math.log(3.0) - 2.3025851 * jax.random.uniform(streams_of[1], (NX, NY, NZ), jnp.float32) ** steps_of(streams_of[1], (NX, NY, NZ), ((0, 8),), -0.2, 0.2)), 0.3, 3.0)
    directions = gaussian(streams_of[2], (DIRS, N_SPACE, CBLOCK), 1.0, 6.0, ((0, 4), (1, 8)), jnp.float32)
    owner_map = jax.random.permutation(streams_of[3], N_DIR).astype(jnp.int32)
    block_map = jax.random.permutation(streams_of[4], N_SPACE).astype(jnp.int32)
    return {"store": store, "rate": rate, "directions": directions, "owner_map": owner_map, "block_map": block_map}


spread_a = 0.08
spread_b = 0.06
drift = 0.25
decay_rate = 0.05
rate_scale = 0.1


def advance(ext, slab, rate, vfine):
    centre = ext[:, 1:-1]
    padded = jnp.pad(centre, ((0, 0), (0, 0), (1, 1), (1, 1)))
    beside = ext[:, 2:] + ext[:, :-2]
    beside = beside + padded[:, :, 2:, 1:-1] + padded[:, :, :-2, 1:-1]
    beside = beside + padded[:, :, 1:-1, 2:] + padded[:, :, 1:-1, :-2]
    laplace = beside - 6.0 * centre
    upwind = centre - ext[:, :-2]
    first, second = centre[0], centre[1]
    conc_a, conc_b = slab[0], slab[1]
    source = rate_scale * rate * (vfine * conc_a * conc_b + first * conc_b + conc_a * second)
    first_new = first + spread_a * laplace[0] - drift * upwind[0] - source
    second_new = second + spread_b * laplace[1] - drift * upwind[1] + source - decay_rate * second
    return jnp.stack([first_new, second_new], 0)


def reference(store, rate, directions, owner_map, block_map):
    chosen = directions[:, block_map]
    coarse = chosen.reshape(DIRS, NX // 2, NY // 4, NZ // 4)

    def one_direction(coarse_one):
        vfine = jnp.repeat(jnp.repeat(jnp.repeat(coarse_one, 2, 0), 4, 1), 4, 2)
        state = jnp.zeros((2, NX, NY, NZ), jnp.float32)
        for step in range(STEPS):
            slab = lax.dynamic_index_in_dim(store, owner_map[step].astype(jnp.int32), 0, keepdims=False)
            for inner in range(SUBSTEPS):
                ext = jnp.pad(state, ((0, 0), (1, 1), (0, 0), (0, 0)))
                state = advance(ext, slab, rate, vfine)
        return state

    tangent = lax.map(one_direction, coarse)
    means = tangent[:, 1].reshape(DIRS, NX // 2, 2, NY // 4, 4, NZ // 4, 4).mean(axis=(2, 4, 6))
    coarse_q = means.reshape(DIRS, N_SPACE, CBLOCK)
    sens = jnp.zeros_like(coarse_q).at[:, block_map].set(coarse_q)
    return (tangent, sens)
```

```python
import functools

import jax
import jax.numpy as jnp
from jax import lax
from jax.experimental import pallas as pl
from jax.experimental.pallas import tpu as pltpu
from jax.sharding import PartitionSpec as P

spread_a = 0.08
spread_b = 0.06
drift = 0.25
decay_rate = 0.05
rate_scale = 0.1

keep_a = 1.0 - 6.0 * spread_a - drift
keep_b = 1.0 - 6.0 * spread_b - drift - decay_rate
back_a = (spread_a + drift) / spread_a
back_b = (spread_b + drift) / spread_b

EDGE = 8
PAD = 8
CHUNK = 24
ANY = pl.BlockSpec(memory_space=pl.ANY)
SMEM = pl.BlockSpec(memory_space=pltpu.SMEM)
VMEM = pl.BlockSpec(memory_space=pltpu.VMEM)


def chunks(rows):
    return [(at, min(CHUNK, rows - at)) for at in range(0, rows, CHUNK)]


def run_all(copies):
    for copy in copies:
        copy.start()
    for copy in copies:
        copy.wait()


def arrange(scal, store, rate, mine, other, rate_m, sems):
    core, odd = scal[0], scal[1]
    rows = mine.shape[2]
    shift = rate.shape[1] // 2 - EDGE
    first = pl.multiple_of(core * shift, 8)
    second = pl.multiple_of((1 - core) * shift, 8)
    copies = []
    for m in range(4):
        layer = jnp.where(odd == 1, 3 - m, m)
        for start, target in ((second, other), (first, mine)):
            copies.append((store.at[0, :, layer, pl.ds(start, rows)], target.at[:, m]))
        copies.append((rate.at[layer, pl.ds(first, rows)], rate_m.at[m]))
    run_all([pltpu.make_async_copy(a, b, sems.at[i]) for i, (a, b) in enumerate(copies)])


def exact_dot(a, b):
    return jnp.dot(a, b, precision=lax.Precision.HIGHEST, preferred_element_type=jnp.float32)


def expand(scal, own, sib, vfine):
    core = scal[0]
    rows = vfine.shape[2]
    shift = rows - 2 * EDGE
    packed = own.shape[3]
    row = lax.broadcasted_iota(jnp.int32, (rows, 4 * packed), 0) + core * shift
    column = lax.broadcasted_iota(jnp.int32, (rows, 4 * packed), 1)
    coarse = row // 4
    pick_rows = (coarse == 4 * (column % packed) + column // packed).astype(jnp.float32)
    lane = lax.broadcasted_iota(jnp.int32, (128, 512), 0)
    z = lax.broadcasted_iota(jnp.int32, (128, 512), 1)
    pick_lanes = (lane == 32 * (z // 128) + (z % 128) // 4).astype(jnp.float32)
    for k in range(8):
        blocks = [(own if d < 2 else sib)[scal[3 + k], d % 2, scal[11 + k]] for d in range(4)]
        wide = exact_dot(jnp.concatenate(blocks, 0), pick_lanes)
        table = jnp.concatenate(
            [
                jnp.concatenate(
                    [wide[packed * d : packed * (d + 1), 128 * j : 128 * (j + 1)] for j in range(4)], 0
                )
                for d in range(4)
            ],
            1,
        )
        filled = exact_dot(pick_rows, table)
        for d in range(4):
            vfine[d, k] = filled[:, 128 * d : 128 * (d + 1)]


def masks(rows):
    lane = lax.broadcasted_iota(jnp.int32, (rows, 128), 1)
    return lane == 0, lane == 127


def around(ref, lead, layer, before, after, at, rows):
    first, last = masks(rows)
    here = ref[lead, layer, pl.ds(PAD + at, rows)]
    total = ref[lead, layer, pl.ds(PAD - 1 + at, rows)] + ref[lead, layer, pl.ds(PAD + 1 + at, rows)]
    total = total + jnp.where(first, 0.0, pltpu.roll(here, 1, 1))
    total = total + jnp.where(last, 0.0, pltpu.roll(here, 127, 1))
    total = total + ref[lead, after, pl.ds(PAD + at, rows)]
    return here, total, ref[lead, before, pl.ds(PAD + at, rows)]


def clear_pads(ref):
    dirs, layers, rows, lanes = ref.shape
    zero = jnp.zeros((dirs, PAD, lanes), jnp.float32)

    @pl.loop(0, layers)
    def _(i):
        ref[:, i, pl.ds(0, PAD)] = zero
        ref[:, i, pl.ds(rows - PAD, PAD)] = zero


def clear_layer(ref, layer):
    ref[:, layer] = jnp.zeros((ref.shape[0], ref.shape[2], ref.shape[3]), jnp.float32)


def update(source, target, field_at, state_at, out_at, sigma, fields, weight, rows):
    p_ref, q_ref = source
    p_out, q_out, pad = target
    for at, n in chunks(rows):
        a = fields[0, field_at, pl.ds(at, n)]
        b = fields[1, field_at, pl.ds(at, n)]
        hold_a = keep_a - b
        hold_b = keep_b + a
        for d in range(4):
            p, p_sum, p_back = around(p_ref, d, state_at, state_at - sigma, state_at + sigma, at, n)
            q, q_sum, q_back = around(q_ref, d, state_at, state_at - sigma, state_at + sigma, at, n)
            w = weight[d, field_at, pl.ds(at, n)]
            p_out[d, out_at, pl.ds(pad + at, n)] = (
                spread_a * (p_sum + back_a * p_back) + hold_a * p - (a * q + w)
            )
            q_out[d, out_at, pl.ds(pad + at, n)] = (
                spread_b * (q_sum + back_b * q_back) + hold_b * q + (b * p + w)
            )


def first_step(
    scal, rate_m, rate_e, rate_l, s_a, s_b, e_a, e_b, l_a, l_b, far_e, far_l, vfine,
    p3, q3, rate, slab, far, v, q1, p2, q2, sems,
):
    sigma = 1 - 2 * scal[1]
    has_late = scal[2]
    rows = rate.shape[1]
    moves = [(rate_m, rate.at[pl.ds(4, 4)])]
    moves += [(s_a, slab.at[:, pl.ds(4, 2)]), (s_b, slab.at[:, pl.ds(6, 2)])]
    for j in range(4):
        moves.append((rate_e.at[j], rate.at[11 - j]))
        moves.append((rate_l.at[j], rate.at[3 - j]))
    for j in range(2):
        moves.append((e_a.at[:, j], slab.at[:, 11 - j]))
        moves.append((e_b.at[:, j], slab.at[:, 9 - j]))
        moves.append((l_a.at[:, j], slab.at[:, 3 - j]))
        moves.append((l_b.at[:, j], slab.at[:, 1 - j]))
    moves += [(far_l, far.at[0]), (far_e, far.at[1]), (vfine, v)]
    copies = [pltpu.make_async_copy(a, b, sems.at[i]) for i, (a, b) in enumerate(moves)]
    for copy in copies:
        copy.start()
    for ref in (q1, p2, q2, p3, q3):
        clear_pads(ref)
    for ref in (p2, q2):
        clear_layer(ref, 3)
    for ref in (p3, q3):
        clear_layer(ref, 2)
    for copy in copies:
        copy.wait()

    for i, (layer, coarse) in enumerate(((0, 0), (13, 7))):
        for at, n in chunks(rows):
            w = far[i, pl.ds(at, n)]
            for d in range(4):
                q1[d, layer, pl.ds(PAD + at, n)] = w * v[d, coarse, pl.ds(at, n)]

    @pl.loop(0, 12)
    def _(i):
        coarse = (i + 2) // 2
        for at, n in chunks(rows):
            scaled = rate_scale * rate[i, pl.ds(at, n)]
            b = slab[1, i, pl.ds(at, n)]
            a = scaled * slab[0, i, pl.ds(at, n)]
            w = a * b
            slab[0, i, pl.ds(at, n)] = a
            slab[1, i, pl.ds(at, n)] = scaled * b
            for d in range(4):
                q1[d, i + 1, pl.ds(PAD + at, n)] = w * v[d, coarse, pl.ds(at, n)]

    @pl.loop(jnp.where(has_late == 1, 0, 4), 12)
    def _(i):
        for at, n in chunks(rows):
            both = slab[0, i, pl.ds(at, n)] - slab[1, i, pl.ds(at, n)]
            hold_a = both + (1.0 + keep_a)
            hold_b = both + (1.0 + keep_b)
            for d in range(4):
                q, total, back = around(q1, d, i + 1, i + 1 - sigma, i + 1 + sigma, at, n)
                p2[d, i, pl.ds(PAD + at, n)] = -(spread_a * (total + back_a * back) + hold_a * q)
                q2[d, i, pl.ds(PAD + at, n)] = spread_b * (total + back_b * back) + hold_b * q

    @pl.loop(jnp.where(has_late == 1, 0, 3), 10)
    def _(i):
        for at, n in chunks(rows):
            a = slab[0, i + 1, pl.ds(at, n)]
            b = slab[1, i + 1, pl.ds(at, n)]
            hold_a = keep_a - b
            hold_b = keep_b + a
            for d in range(4):
                p, p_sum, p_back = around(p2, d, i + 1, i + 1 - sigma, i + 1 + sigma, at, n)
                q, q_sum, q_back = around(q2, d, i + 1, i + 1 - sigma, i + 1 + sigma, at, n)
                w = q1[d, i + 2, pl.ds(PAD + at, n)]
                p3[d, i, pl.ds(PAD + at, n)] = (
                    spread_a * (p_sum + back_a * p_back) + hold_a * p - (a * q + w)
                )
                q3[d, i, pl.ds(PAD + at, n)] = (
                    spread_b * (q_sum + back_b * q_back) + hold_b * q + (b * p + w)
                )


def second_step(
    scal, rate_m, rate_e, rate_l, s_a, s_b, e_b, l_a, vfine, p3_in, q3_in,
    tangent, sent, means, rate, slab, v, p3, q3, weight, p4, q4, p5, q5, p6, q6, sems, out_sems,
):
    core, odd, has_late = scal[0], scal[1], scal[2]
    sigma = 1 - 2 * odd
    rows = rate.shape[1]
    half = rows - EDGE
    moves = [(p3_in, p3), (q3_in, q3), (rate_m, rate.at[pl.ds(2, 4)])]
    moves += [(s_a, slab.at[:, pl.ds(2, 2)]), (s_b, slab.at[:, pl.ds(4, 2)])]
    for j in range(2):
        moves.append((rate_e.at[3 - j], rate.at[6 + j]))
        moves.append((rate_l.at[j], rate.at[1 - j]))
        moves.append((e_b.at[:, 1 - j], slab.at[:, 6 + j]))
        moves.append((l_a.at[:, j], slab.at[:, 1 - j]))
    moves.append((vfine.at[:, pl.ds(2, 4)], v))
    copies = [pltpu.make_async_copy(a, b, sems.at[i]) for i, (a, b) in enumerate(moves)]
    for copy in copies:
        copy.start()
    for ref in (p4, q4, p5, q5):
        clear_pads(ref)
    for ref in (p4, q4):
        clear_layer(ref, 1)
    for ref in (p5, q5):
        clear_layer(ref, 0)
    for copy in copies:
        copy.wait()

    @pl.loop(0, 8)
    def _(i):
        coarse = i // 2
        for at, n in chunks(rows):
            scaled = rate_scale * rate[i, pl.ds(at, n)]
            b = slab[1, i, pl.ds(at, n)]
            a = scaled * slab[0, i, pl.ds(at, n)]
            w = a * b
            slab[0, i, pl.ds(at, n)] = a
            slab[1, i, pl.ds(at, n)] = scaled * b
            for d in range(4):
                weight[d, i, pl.ds(at, n)] = w * v[d, coarse, pl.ds(at, n)]

    @pl.loop(jnp.where(has_late == 1, 0, 2), 8)
    def _(i):
        update((p3, q3), (p4, q4, PAD), i, i + 1, i, sigma, slab, weight, rows)

    @pl.loop(jnp.where(has_late == 1, 0, 1), 6)
    def _(i):
        update((p4, q4), (p5, q5, PAD), i + 1, i + 1, i, sigma, slab, weight, rows)

    start = pl.multiple_of(core * EDGE, 8)
    place = pl.multiple_of(core * half, 8)

    def writes(i):
        layer = jnp.where(odd == 1, 3 - i, i)
        for j, ref in enumerate((p6, q6)):
            yield pltpu.make_async_copy(
                ref.at[pl.ds(0, 2), i, pl.ds(start, half)],
                tangent.at[:, j, layer, pl.ds(place, half)],
                out_sems.at[i, j],
            )
            yield pltpu.make_async_copy(
                ref.at[pl.ds(2, 2), i, pl.ds(start, half)],
                sent.at[:, j, layer],
                out_sems.at[i, 2 + j],
            )

    @pl.loop(0, 4)
    def _(i):
        update((p5, q5), (p6, q6, 0), i + 2, i + 1, i, sigma, slab, weight, rows)
        for copy in writes(i):
            copy.start()

    packed = half // 16
    row = lax.broadcasted_iota(jnp.int32, (4 * packed, half), 0)
    column = lax.broadcasted_iota(jnp.int32, (4 * packed, half), 1)
    sum_rows = (column // 4 == 4 * (row % packed) + row // packed).astype(jnp.float32)
    lane = lax.broadcasted_iota(jnp.int32, (512, 128), 1)
    z = lax.broadcasted_iota(jnp.int32, (512, 128), 0)
    sum_lanes = (lane == 32 * (z // 128) + (z % 128) // 4).astype(jnp.float32)
    pairs = [
        q6[d, 2 * k, pl.ds(start, half)] + q6[d, 2 * k + 1, pl.ds(start, half)]
        for d in range(4)
        for k in range(2)
    ]
    summed = exact_dot(sum_rows, jnp.concatenate(pairs, 1))
    spread = jnp.concatenate(
        [
            jnp.concatenate(
                [summed[packed * j : packed * (j + 1), 128 * i : 128 * (i + 1)] for j in range(4)], 1
            )
            for i in range(8)
        ],
        0,
    )
    total = exact_dot(spread, sum_lanes) * (1.0 / 32.0)
    for d in range(4):
        for k in range(2):
            layer = jnp.where(odd == 1, 1 - k, k)
            means[d, layer] = total[packed * (2 * d + k) : packed * (2 * d + k + 1)]

    @pl.loop(0, 4)
    def _(i):
        for copy in writes(i):
            copy.wait()


def finish(scal, held, received, tangent, stage, sems):
    half = received.shape[3]
    place = pl.multiple_of((1 - scal[0]) * half, 8)
    parts = [(i, j) for i in range(2) for j in range(2)]
    loads = [
        pltpu.make_async_copy(received.at[i, j], stage.at[i, j], sems.at[0, 2 * i + j]) for i, j in parts
    ]
    stores = [
        pltpu.make_async_copy(
            stage.at[i, j], tangent.at[i, j, :, pl.ds(place, half)], sems.at[1, 2 * i + j]
        )
        for i, j in parts
    ]
    for copy in loads:
        copy.start()
    for load, store in zip(loads, stores):
        load.wait()
        store.start()
    for copy in stores:
        copy.wait()


def cost(flops, moved):
    return pl.CostEstimate(flops=flops, bytes_accessed=moved, transcendentals=0)


def params(megabytes):
    return pltpu.CompilerParams(vmem_limit_bytes=megabytes << 20)


def shape(*dims):
    return jax.ShapeDtypeStruct(dims, jnp.float32)


def local(store, rate, directions, owner_map, block_map):
    layers, width_y, width_z = rate.shape
    half = width_y // 2
    rows = half + EDGE
    n_space = lax.axis_size("space")
    mine = lax.axis_index("space")
    group = lax.axis_index("dir")
    core, column = group % 2, group // 2
    odd = mine % 2
    has_late = ((mine > 0) & (mine < n_space - 1)).astype(jnp.int32)

    across_core = [(i, i ^ 1) for i in range(4)]
    across_column = [(i, i ^ 2) for i in range(4)]
    swap = [(i, i ^ 1) for i in range(n_space)]
    ahead = [(i, i + 2) for i in range(0, n_space - 2, 2)] + [(i, i - 2) for i in range(3, n_space, 2)]
    behind = [(b, a) for a, b in ahead]
    to_core = functools.partial(lax.ppermute, axis_name="dir", perm=across_core)
    to_column = functools.partial(lax.ppermute, axis_name="dir", perm=across_column)
    to_pair = functools.partial(lax.ppermute, axis_name="space", perm=swap)
    to_ahead = functools.partial(lax.ppermute, axis_name="space", perm=ahead)
    to_behind = functools.partial(lax.ppermute, axis_name="space", perm=behind)

    gathered = directions.reshape(1, 2, 2, 32, 128)
    reach = 1
    while reach < n_space:
        pairs = [(i, i ^ reach) for i in range(n_space)]
        gathered = jnp.concatenate([gathered, lax.ppermute(gathered, "space", pairs)], 0)
        reach *= 2
    gathered_sib = to_core(gathered)
    local_coarse = jnp.arange(8, dtype=jnp.int32) - 3
    coarse_at = 2 * mine + jnp.where(odd == 1, 1 - local_coarse, local_coarse)
    block = jnp.clip(coarse_at // 2, 0, n_space - 1)
    scal = jnp.concatenate(
        [
            jnp.stack([core, odd, has_late]).astype(jnp.int32),
            (block_map[block] ^ mine).astype(jnp.int32),
            (coarse_at % 2).astype(jnp.int32),
        ]
    )

    own, other, rate_m = pl.pallas_call(
        arrange,
        out_shape=(shape(2, 4, rows, width_z), shape(2, 4, rows, width_z), shape(4, rows, width_z)),
        in_specs=[SMEM, ANY, ANY],
        out_specs=[VMEM] * 3,
        cost_estimate=cost(0, 6 << 20),
        scratch_shapes=[pltpu.SemaphoreType.DMA((12,))],
        name="arrange",
    )(scal, store, rate)
    received = to_core(other)
    rate_e = to_pair(rate_m)
    rate_l = to_ahead(rate_e)

    def slab(step):
        owner = owner_map[step]
        parts = []
        for at in (0, 2):
            have = jnp.where(group == owner, own[:, at : at + 2], received[:, at : at + 2])
            came = to_column(have)
            parts.append(jnp.where(column == owner // 2, have, came))
        return parts

    s0_a, s0_b = slab(0)
    e0_a = to_pair(s0_a)
    e0_b = to_pair(s0_b)
    l0_a = to_ahead(e0_a)
    l0_b = to_ahead(e0_b)
    w_near = rate_scale * rate_m[0] * s0_a[0, 0] * s0_a[1, 0]
    w_late = rate_scale * rate_m[3] * s0_b[0, 1] * s0_b[1, 1]
    far_e = to_behind(w_near)
    far_l = to_ahead(w_late)
    s1_a, s1_b = slab(1)
    e1_a = to_pair(s1_a)
    l1_a = to_ahead(e1_a)
    e1_b = to_pair(s1_b)

    vfine = pl.pallas_call(
        expand,
        out_shape=shape(4, 8, rows, width_z),
        in_specs=[SMEM, VMEM, VMEM],
        out_specs=VMEM,
        name="expand",
        cost_estimate=cost(0, 25 << 20),
        compiler_params=params(32),
    )(scal, gathered, gathered_sib)

    tall = rows + 2 * PAD

    def vmem(*dims):
        return pltpu.VMEM(dims, jnp.float32)

    p3, q3 = pl.pallas_call(
        first_step,
        out_shape=(shape(4, 10, tall, width_z),) * 2,
        in_specs=[SMEM] + [ANY] * 12,
        out_specs=[VMEM] * 2,
        scratch_shapes=[
            vmem(12, rows, width_z),
            vmem(2, 12, rows, width_z),
            vmem(2, rows, width_z),
            vmem(4, 8, rows, width_z),
            vmem(4, 14, tall, width_z),
            vmem(4, 12, tall, width_z),
            vmem(4, 12, tall, width_z),
            pltpu.SemaphoreType.DMA((22,)),
        ],
        name="first_step",
        cost_estimate=cost(0, 50 << 20),
        compiler_params=params(50),
    )(scal, rate_m, rate_e, rate_l, s0_a, s0_b, e0_a, e0_b, l0_a, l0_b, far_e, far_l, vfine)

    tangent, sent, means = pl.pallas_call(
        second_step,
        out_shape=(
            shape(2, 2, 4, width_y, width_z),
            shape(2, 2, 4, half, width_z),
            shape(4, 2, half // 16, 128),
        ),
        in_specs=[SMEM] + [ANY] * 10,
        out_specs=[ANY, ANY, VMEM],
        scratch_shapes=[
            vmem(8, rows, width_z),
            vmem(2, 8, rows, width_z),
            vmem(4, 4, rows, width_z),
            vmem(4, 10, tall, width_z),
            vmem(4, 10, tall, width_z),
            vmem(4, 8, rows, width_z),
            vmem(4, 8, tall, width_z),
            vmem(4, 8, tall, width_z),
            vmem(4, 6, tall, width_z),
            vmem(4, 6, tall, width_z),
            vmem(4, 4, rows, width_z),
            vmem(4, 4, rows, width_z),
            pltpu.SemaphoreType.DMA((14,)),
            pltpu.SemaphoreType.DMA((4, 4)),
        ],
        name="second_step",
        cost_estimate=cost(0, 55 << 20),
        compiler_params=params(56),
    )(scal, rate_m, rate_e, rate_l, s1_a, s1_b, e1_b, l1_a, vfine, p3, q3)

    first, second = means[:2], means[2:]

    def joined(a, b):
        return jnp.where(core == 0, jnp.concatenate([a, b], 2), jnp.concatenate([b, a], 2))

    both = [(i * n_space + j, (i ^ 1) * n_space + (j ^ 1)) for i in range(4) for j in range(n_space)]
    here = joined(first, to_core(second))
    there = joined(to_pair(first), lax.ppermute(second, ("dir", "space"), both))
    partner = mine ^ 1
    source = jnp.argmax(block_map == mine).astype(jnp.int32)
    sens = jnp.where(source == mine, here, there)
    for j in range(2, n_space, 2):
        target = mine ^ j
        row = jnp.where(block_map[mine] == target, here, there)
        pairs = [(i, i ^ j) for i in range(n_space)]
        came = lax.ppermute(row, "space", pairs)
        sens = jnp.where(source // 2 == target // 2, came, sens)

    tangent = pl.pallas_call(
        finish,
        out_shape=shape(2, 2, 4, width_y, width_z),
        in_specs=[SMEM, ANY, ANY],
        out_specs=ANY,
        scratch_shapes=[vmem(2, 2, 4, half, width_z), pltpu.SemaphoreType.DMA((2, 4))],
        input_output_aliases={1: 0},
        cost_estimate=cost(0, 2 << 22),
        name="finish",
    )(scal, tangent, to_core(sent))
    return tangent, sens.reshape(2, 1, -1)


def solution(mesh):
    return jax.shard_map(
        local,
        mesh=mesh,
        in_specs=(
            P("dir", None, "space", None, None),
            P("space", None, None),
            P("dir", "space", None),
            P(),
            P(),
        ),
        out_specs=(P("dir", None, "space", None, None), P("dir", "space", None)),
        check_vma=False,
    )
```

```python
import functools

import jax
import jax.numpy as jnp
from jax import lax
from jax.experimental import pallas as pl
from jax.experimental.pallas import tpu as pltpu
from jax.sharding import PartitionSpec as P

spread_a = 0.08
spread_b = 0.06
drift = 0.25
decay_rate = 0.05
rate_scale = 0.1

keep_a = 1.0 - 6.0 * spread_a - drift
keep_b = 1.0 - 6.0 * spread_b - drift - decay_rate
back_a = (spread_a + drift) / spread_a
back_b = (spread_b + drift) / spread_b

EDGE = 8
PAD = 8
CHUNK = 24
ANY = pl.BlockSpec(memory_space=pl.ANY)
SMEM = pl.BlockSpec(memory_space=pltpu.SMEM)
VMEM = pl.BlockSpec(memory_space=pltpu.VMEM)


def chunks(rows):
    return [(at, min(CHUNK, rows - at)) for at in range(0, rows, CHUNK)]


def run_all(copies):
    for copy in copies:
        copy.start()
    for copy in copies:
        copy.wait()


def arrange(scal, store, rate, mine, other, rate_m, sems):
    core, odd = scal[0], scal[1]
    rows = mine.shape[2]
    shift = rate.shape[1] // 2 - EDGE
    first = pl.multiple_of(core * shift, 8)
    second = pl.multiple_of((1 - core) * shift, 8)
    copies = []
    for m in range(4):
        layer = jnp.where(odd == 1, 3 - m, m)
        for start, target in ((second, other), (first, mine)):
            copies.append((store.at[0, :, layer, pl.ds(start, rows)], target.at[:, m]))
        copies.append((rate.at[layer, pl.ds(first, rows)], rate_m.at[m]))
    run_all([pltpu.make_async_copy(a, b, sems.at[i]) for i, (a, b) in enumerate(copies)])


def exact_dot(a, b):
    return jnp.dot(a, b, precision=lax.Precision.HIGHEST, preferred_element_type=jnp.float32)


def expand(scal, own, sib, vfine):
    core = scal[0]
    rows = vfine.shape[2]
    shift = rows - 2 * EDGE
    packed = own.shape[3]
    row = lax.broadcasted_iota(jnp.int32, (rows, 4 * packed), 0) + core * shift
    column = lax.broadcasted_iota(jnp.int32, (rows, 4 * packed), 1)
    coarse = row // 4
    pick_rows = (coarse == 4 * (column % packed) + column // packed).astype(jnp.float32)
    lane = lax.broadcasted_iota(jnp.int32, (128, 512), 0)
    z = lax.broadcasted_iota(jnp.int32, (128, 512), 1)
    pick_lanes = (lane == 32 * (z // 128) + (z % 128) // 4).astype(jnp.float32)
    for k in range(8):
        blocks = [(own if d < 2 else sib)[scal[3 + k], d % 2, scal[11 + k]] for d in range(4)]
        wide = exact_dot(jnp.concatenate(blocks, 0), pick_lanes)
        table = jnp.concatenate(
            [
                jnp.concatenate(
                    [wide[packed * d : packed * (d + 1), 128 * j : 128 * (j + 1)] for j in range(4)], 0
                )
                for d in range(4)
            ],
            1,
        )
        filled = exact_dot(pick_rows, table)
        for d in range(4):
            vfine[d, k] = filled[:, 128 * d : 128 * (d + 1)]


def masks(rows):
    lane = lax.broadcasted_iota(jnp.int32, (rows, 128), 1)
    return lane == 0, lane == 127


def around(ref, lead, layer, before, after, at, rows):
    first, last = masks(rows)
    here = ref[lead, layer, pl.ds(PAD + at, rows)]
    total = ref[lead, layer, pl.ds(PAD - 1 + at, rows)] + ref[lead, layer, pl.ds(PAD + 1 + at, rows)]
    total = total + jnp.where(first, 0.0, pltpu.roll(here, 1, 1))
    total = total + jnp.where(last, 0.0, pltpu.roll(here, 127, 1))
    total = total + ref[lead, after, pl.ds(PAD + at, rows)]
    return here, total, ref[lead, before, pl.ds(PAD + at, rows)]


def clear_pads(ref):
    dirs, layers, rows, lanes = ref.shape
    zero = jnp.zeros((dirs, PAD, lanes), jnp.float32)

    @pl.loop(0, layers)
    def _(i):
        ref[:, i, pl.ds(0, PAD)] = zero
        ref[:, i, pl.ds(rows - PAD, PAD)] = zero


def clear_layer(ref, layer):
    ref[:, layer] = jnp.zeros((ref.shape[0], ref.shape[2], ref.shape[3]), jnp.float32)


def update(source, target, field_at, state_at, out_at, sigma, fields, weight, rows):
    p_ref, q_ref = source
    p_out, q_out, pad = target
    for at, n in chunks(rows):
        a = fields[0, field_at, pl.ds(at, n)]
        b = fields[1, field_at, pl.ds(at, n)]
        hold_a = keep_a - b
        hold_b = keep_b + a
        for d in range(4):
            p, p_sum, p_back = around(p_ref, d, state_at, state_at - sigma, state_at + sigma, at, n)
            q, q_sum, q_back = around(q_ref, d, state_at, state_at - sigma, state_at + sigma, at, n)
            w = weight[d, field_at, pl.ds(at, n)]
            p_out[d, out_at, pl.ds(pad + at, n)] = (
                spread_a * (p_sum + back_a * p_back) + hold_a * p - (a * q + w)
            )
            q_out[d, out_at, pl.ds(pad + at, n)] = (
                spread_b * (q_sum + back_b * q_back) + hold_b * q + (b * p + w)
            )


def first_step(
    scal, rate_m, rate_e, rate_l, s_a, s_b, e_a, e_b, l_a, l_b, far_e, far_l, v,
    state, rate, slab, far, q1, p2, q2, sems,
):
    sigma = 1 - 2 * scal[1]
    has_late = scal[2]
    p3, q3 = state.at[0], state.at[1]
    rows = rate.shape[1]
    moves = [(rate_m, rate.at[pl.ds(4, 4)])]
    moves += [(s_a, slab.at[:, pl.ds(4, 2)]), (s_b, slab.at[:, pl.ds(6, 2)])]
    for j in range(4):
        moves.append((rate_e.at[j], rate.at[11 - j]))
        moves.append((rate_l.at[j], rate.at[3 - j]))
    for j in range(2):
        moves.append((e_a.at[:, j], slab.at[:, 11 - j]))
        moves.append((e_b.at[:, j], slab.at[:, 9 - j]))
        moves.append((l_a.at[:, j], slab.at[:, 3 - j]))
        moves.append((l_b.at[:, j], slab.at[:, 1 - j]))
    moves += [(far_l, far.at[0]), (far_e, far.at[1])]
    copies = [pltpu.make_async_copy(a, b, sems.at[i]) for i, (a, b) in enumerate(moves)]
    for copy in copies:
        copy.start()
    for ref in (q1, p2, q2, p3, q3):
        clear_pads(ref)
    for ref in (p2, q2):
        clear_layer(ref, 3)
    for ref in (p3, q3):
        clear_layer(ref, 2)
    for copy in copies:
        copy.wait()

    for i, (layer, coarse) in enumerate(((0, 0), (13, 7))):
        for at, n in chunks(rows):
            w = far[i, pl.ds(at, n)]
            for d in range(4):
                q1[d, layer, pl.ds(PAD + at, n)] = w * v[d, coarse, pl.ds(at, n)]

    @pl.loop(0, 12)
    def _(i):
        coarse = (i + 2) // 2
        for at, n in chunks(rows):
            scaled = rate_scale * rate[i, pl.ds(at, n)]
            b = slab[1, i, pl.ds(at, n)]
            a = scaled * slab[0, i, pl.ds(at, n)]
            w = a * b
            slab[0, i, pl.ds(at, n)] = a
            slab[1, i, pl.ds(at, n)] = scaled * b
            for d in range(4):
                q1[d, i + 1, pl.ds(PAD + at, n)] = w * v[d, coarse, pl.ds(at, n)]

    @pl.loop(jnp.where(has_late == 1, 0, 4), 12)
    def _(i):
        for at, n in chunks(rows):
            both = slab[0, i, pl.ds(at, n)] - slab[1, i, pl.ds(at, n)]
            hold_a = both + (1.0 + keep_a)
            hold_b = both + (1.0 + keep_b)
            for d in range(4):
                q, total, back = around(q1, d, i + 1, i + 1 - sigma, i + 1 + sigma, at, n)
                p2[d, i, pl.ds(PAD + at, n)] = -(spread_a * (total + back_a * back) + hold_a * q)
                q2[d, i, pl.ds(PAD + at, n)] = spread_b * (total + back_b * back) + hold_b * q

    @pl.loop(jnp.where(has_late == 1, 0, 3), 10)
    def _(i):
        for at, n in chunks(rows):
            a = slab[0, i + 1, pl.ds(at, n)]
            b = slab[1, i + 1, pl.ds(at, n)]
            hold_a = keep_a - b
            hold_b = keep_b + a
            for d in range(4):
                p, p_sum, p_back = around(p2, d, i + 1, i + 1 - sigma, i + 1 + sigma, at, n)
                q, q_sum, q_back = around(q2, d, i + 1, i + 1 - sigma, i + 1 + sigma, at, n)
                w = q1[d, i + 2, pl.ds(PAD + at, n)]
                p3[d, i, pl.ds(PAD + at, n)] = (
                    spread_a * (p_sum + back_a * p_back) + hold_a * p - (a * q + w)
                )
                q3[d, i, pl.ds(PAD + at, n)] = (
                    spread_b * (q_sum + back_b * q_back) + hold_b * q + (b * p + w)
                )


def second_step(
    scal, rate_m, rate_e, rate_l, s_a, s_b, e_b, l_a, v, state,
    tangent, sent, means, rate, slab, weight, p4, q4, p5, q5, p6, q6, sems, out_sems,
):
    core, odd, has_late = scal[0], scal[1], scal[2]
    sigma = 1 - 2 * odd
    rows = rate.shape[1]
    half = rows - EDGE
    p3, q3 = state.at[0], state.at[1]
    moves = [(rate_m, rate.at[pl.ds(2, 4)])]
    moves += [(s_a, slab.at[:, pl.ds(2, 2)]), (s_b, slab.at[:, pl.ds(4, 2)])]
    for j in range(2):
        moves.append((rate_e.at[3 - j], rate.at[6 + j]))
        moves.append((rate_l.at[j], rate.at[1 - j]))
        moves.append((e_b.at[:, 1 - j], slab.at[:, 6 + j]))
        moves.append((l_a.at[:, j], slab.at[:, 1 - j]))
    copies = [pltpu.make_async_copy(a, b, sems.at[i]) for i, (a, b) in enumerate(moves)]
    for copy in copies:
        copy.start()
    for ref in (p4, q4, p5, q5):
        clear_pads(ref)
    for ref in (p4, q4):
        clear_layer(ref, 1)
    for ref in (p5, q5):
        clear_layer(ref, 0)
    for copy in copies:
        copy.wait()

    @pl.loop(0, 8)
    def _(i):
        coarse = i // 2 + 2
        for at, n in chunks(rows):
            scaled = rate_scale * rate[i, pl.ds(at, n)]
            b = slab[1, i, pl.ds(at, n)]
            a = scaled * slab[0, i, pl.ds(at, n)]
            w = a * b
            slab[0, i, pl.ds(at, n)] = a
            slab[1, i, pl.ds(at, n)] = scaled * b
            for d in range(4):
                weight[d, i, pl.ds(at, n)] = w * v[d, coarse, pl.ds(at, n)]

    @pl.loop(jnp.where(has_late == 1, 0, 2), 8)
    def _(i):
        update((p3, q3), (p4, q4, PAD), i, i + 1, i, sigma, slab, weight, rows)

    @pl.loop(jnp.where(has_late == 1, 0, 1), 6)
    def _(i):
        update((p4, q4), (p5, q5, PAD), i + 1, i + 1, i, sigma, slab, weight, rows)

    start = pl.multiple_of(core * EDGE, 8)
    place = pl.multiple_of(core * half, 8)

    def writes(i):
        layer = jnp.where(odd == 1, 3 - i, i)
        for j, ref in enumerate((p6, q6)):
            yield pltpu.make_async_copy(
                ref.at[pl.ds(0, 2), i, pl.ds(start, half)],
                tangent.at[:, j, layer, pl.ds(place, half)],
                out_sems.at[i, j],
            )
            yield pltpu.make_async_copy(
                ref.at[pl.ds(2, 2), i, pl.ds(start, half)],
                sent.at[:, j, layer],
                out_sems.at[i, 2 + j],
            )

    @pl.loop(0, 4)
    def _(i):
        update((p5, q5), (p6, q6, 0), i + 2, i + 1, i, sigma, slab, weight, rows)
        for copy in writes(i):
            copy.start()

    packed = half // 16
    row = lax.broadcasted_iota(jnp.int32, (4 * packed, half), 0)
    column = lax.broadcasted_iota(jnp.int32, (4 * packed, half), 1)
    sum_rows = (column // 4 == 4 * (row % packed) + row // packed).astype(jnp.float32)
    lane = lax.broadcasted_iota(jnp.int32, (512, 128), 1)
    z = lax.broadcasted_iota(jnp.int32, (512, 128), 0)
    sum_lanes = (lane == 32 * (z // 128) + (z % 128) // 4).astype(jnp.float32)
    pairs = [
        q6[d, 2 * k, pl.ds(start, half)] + q6[d, 2 * k + 1, pl.ds(start, half)]
        for d in range(4)
        for k in range(2)
    ]
    summed = exact_dot(sum_rows, jnp.concatenate(pairs, 1))
    spread = jnp.concatenate(
        [
            jnp.concatenate(
                [summed[packed * j : packed * (j + 1), 128 * i : 128 * (i + 1)] for j in range(4)], 1
            )
            for i in range(8)
        ],
        0,
    )
    total = exact_dot(spread, sum_lanes) * (1.0 / 32.0)
    for d in range(4):
        for k in range(2):
            layer = jnp.where(odd == 1, 1 - k, k)
            means[d, layer] = total[packed * (2 * d + k) : packed * (2 * d + k + 1)]

    @pl.loop(0, 4)
    def _(i):
        for copy in writes(i):
            copy.wait()


def finish(scal, held, received, tangent, sems):
    half = received.shape[3]
    place = pl.multiple_of((1 - scal[0]) * half, 8)
    run_all(
        [
            pltpu.make_async_copy(
                received.at[i, j], tangent.at[i, j, :, pl.ds(place, half)], sems.at[i, j]
            )
            for i in range(2)
            for j in range(2)
        ]
    )


def cost(flops, moved):
    return pl.CostEstimate(flops=flops, bytes_accessed=moved, transcendentals=0)


def after(value, *others):
    return lax.optimization_barrier((value, *others))[0]


def params(megabytes):
    return pltpu.CompilerParams(vmem_limit_bytes=megabytes << 20)


def stay(value):
    return pltpu.with_memory_space_constraint(value, pltpu.VMEM)


def vmem(*dims):
    return pltpu.VMEM(dims, jnp.float32)


def shape(*dims):
    return jax.ShapeDtypeStruct(dims, jnp.float32)


def local(store, rate, directions, owner_map, block_map):
    layers, width_y, width_z = rate.shape
    half = width_y // 2
    rows = half + EDGE
    n_space = lax.axis_size("space")
    mine = lax.axis_index("space")
    group = lax.axis_index("dir")
    core, column = group % 2, group // 2
    odd = mine % 2
    has_late = ((mine > 0) & (mine < n_space - 1)).astype(jnp.int32)
    scal = jnp.stack([core, odd, has_late]).astype(jnp.int32)

    across_core = [(i, i ^ 1) for i in range(4)]
    across_column = [(i, i ^ 2) for i in range(4)]
    swap = [(i, i ^ 1) for i in range(n_space)]
    ahead = [(i, i + 2) for i in range(0, n_space - 2, 2)] + [(i, i - 2) for i in range(3, n_space, 2)]
    behind = [(b, a) for a, b in ahead]
    to_core = functools.partial(lax.ppermute, axis_name="dir", perm=across_core)
    to_column = functools.partial(lax.ppermute, axis_name="dir", perm=across_column)
    to_pair = functools.partial(lax.ppermute, axis_name="space", perm=swap)
    to_ahead = functools.partial(lax.ppermute, axis_name="space", perm=ahead)
    to_behind = functools.partial(lax.ppermute, axis_name="space", perm=behind)

    own, other, rate_m = pl.pallas_call(
        arrange,
        out_shape=(shape(2, 4, rows, width_z), shape(2, 4, rows, width_z), shape(4, rows, width_z)),
        in_specs=[SMEM, ANY, ANY],
        out_specs=[VMEM] * 3,
        cost_estimate=cost(0, 6 << 20),
        scratch_shapes=[pltpu.SemaphoreType.DMA((12,))],
        name="arrange",
    )(scal, store, rate)
    with jax.named_scope("store_core"):
        received = to_core(other)
    gathered = after(directions, rate_m).reshape(1, 2, 2, 32, 128)
    reach = 1
    while reach < n_space:
        pairs = [(i, i ^ reach) for i in range(n_space)]
        with jax.named_scope("directions_space"):
            gathered = jnp.concatenate([gathered, lax.ppermute(gathered, "space", pairs)], 0)
        if reach == 1:
            near = gathered
        reach *= 2
    with jax.named_scope("directions_core"):
        gathered_sib = to_core(gathered)
    local_coarse = jnp.arange(8, dtype=jnp.int32) - 3
    coarse_at = 2 * mine + jnp.where(odd == 1, 1 - local_coarse, local_coarse)
    block = jnp.clip(coarse_at // 2, 0, n_space - 1)
    coarse_scal = jnp.concatenate(
        [scal, (block_map[block] ^ mine).astype(jnp.int32), (coarse_at % 2).astype(jnp.int32)]
    )

    vfine = pl.pallas_call(
        expand,
        out_shape=vmem(4, 8, rows, width_z),
        in_specs=[SMEM, VMEM, VMEM],
        out_specs=VMEM,
        name="expand",
        cost_estimate=cost(0, 25 << 20),
        compiler_params=params(16),
    )(coarse_scal, gathered, gathered_sib)
    with jax.named_scope("rate_pair"):
        rate_e = to_pair(after(rate_m, near))
    with jax.named_scope("rate_ahead"):
        rate_l = to_ahead(after(rate_e, gathered))

    def candidates(step, received):
        owner = owner_map[step]
        return [jnp.where(group == owner, own[:, at : at + 2], received[:, at : at + 2]) for at in (0, 2)]

    def settled(step, have, came):
        return jnp.where(column == owner_map[step] // 2, have, came)

    have0_a, have0_b = candidates(0, received)
    with jax.named_scope("slab0_column"):
        came0_a = to_column(have0_a)
        came0_b = to_column(after(have0_b, came0_a))
    have1_a, have1_b = candidates(1, after(received, have0_a, rate_e))
    s0_a = settled(0, have0_a, came0_a)
    with jax.named_scope("slab0_pair"):
        e0_a = to_pair(after(s0_a, rate_e))
    s0_b = settled(0, have0_b, came0_b)
    w_near = rate_scale * rate_m[0] * s0_a[0, 0] * s0_a[1, 0]
    w_late = rate_scale * rate_m[3] * s0_b[0, 1] * s0_b[1, 1]
    with jax.named_scope("far_layers"):
        far_e = to_behind(w_near)
        far_l = to_ahead(w_late)
    with jax.named_scope("slab1_column"):
        came1_a = to_column(after(have1_a, came0_b, vfine))
        came1_b = to_column(after(have1_b, came1_a, far_e, far_l))
    with jax.named_scope("slab0_pair"):
        e0_b = to_pair(after(s0_b, e0_a))
    with jax.named_scope("slab0_ahead"):
        l0_a = to_ahead(after(e0_a, rate_l))
        l0_b = to_ahead(after(e0_b, l0_a))
    s1_a = settled(1, have1_a, came1_a)
    with jax.named_scope("slab1_pair"):
        e1_a = to_pair(after(s1_a, e0_b))
    with jax.named_scope("slab1_ahead"):
        l1_a = to_ahead(after(e1_a, l0_b))
    s1_b = settled(1, have1_b, came1_b)
    with jax.named_scope("slab1_pair"):
        e1_b = to_pair(after(s1_b, e1_a))
    l0_b = after(l0_b, s1_b, e1_a)

    tall = rows + 2 * PAD
    state = pl.pallas_call(
        first_step,
        out_shape=vmem(2, 4, 10, tall, width_z),
        in_specs=[SMEM] + [ANY] * 11 + [VMEM],
        out_specs=VMEM,
        scratch_shapes=[
            vmem(12, rows, width_z),
            vmem(2, 12, rows, width_z),
            vmem(2, rows, width_z),
            vmem(4, 14, tall, width_z),
            vmem(4, 12, tall, width_z),
            vmem(4, 12, tall, width_z),
            pltpu.SemaphoreType.DMA((21,)),
        ],
        name="first_step",
        cost_estimate=cost(0, 50 << 20),
        compiler_params=params(31),
    )(scal, rate_m, rate_e, rate_l, s0_a, s0_b, e0_a, e0_b, l0_a, l0_b, far_e, far_l, stay(vfine))

    tangent, sent, means = pl.pallas_call(
        second_step,
        out_shape=(
            shape(2, 2, 4, width_y, width_z),
            shape(2, 2, 4, half, width_z),
            shape(4, 2, half // 16, 128),
        ),
        in_specs=[SMEM] + [ANY] * 7 + [VMEM] * 2,
        out_specs=[ANY, ANY, VMEM],
        scratch_shapes=[
            vmem(8, rows, width_z),
            vmem(2, 8, rows, width_z),
            vmem(4, 8, rows, width_z),
            vmem(4, 8, tall, width_z),
            vmem(4, 8, tall, width_z),
            vmem(4, 6, tall, width_z),
            vmem(4, 6, tall, width_z),
            vmem(4, 4, rows, width_z),
            vmem(4, 4, rows, width_z),
            pltpu.SemaphoreType.DMA((11,)),
            pltpu.SemaphoreType.DMA((4, 4)),
        ],
        name="second_step",
        cost_estimate=cost(0, 55 << 20),
        compiler_params=params(36),
    )(scal, rate_m, rate_e, rate_l, s1_a, s1_b, e1_b, l1_a, stay(vfine), stay(state))

    first, second = means[:2], means[2:]
    with jax.named_scope("tangent_core"):
        rest = to_core(sent)

    def joined(a, b):
        return jnp.where(core == 0, jnp.concatenate([a, b], 2), jnp.concatenate([b, a], 2))

    both = [(i * n_space + j, (i ^ 1) * n_space + (j ^ 1)) for i in range(4) for j in range(n_space)]
    here = joined(first, to_core(second))
    there = joined(to_pair(first), lax.ppermute(second, ("dir", "space"), both))
    source = jnp.argmax(block_map == mine).astype(jnp.int32)
    sens = jnp.where(source == mine, here, there)
    came = []
    for j in range(2, n_space, 2):
        row = jnp.where(block_map[mine] == mine ^ j, here, there)
        pairs = [(i, i ^ j) for i in range(n_space)]
        with jax.named_scope("means_space"):
            came.append(lax.ppermute(row, "space", pairs))
    tangent = pl.pallas_call(
        finish,
        out_shape=shape(2, 2, 4, width_y, width_z),
        in_specs=[SMEM, ANY, VMEM],
        out_specs=ANY,
        scratch_shapes=[pltpu.SemaphoreType.DMA((2, 2))],
        input_output_aliases={1: 0},
        cost_estimate=cost(0, 2 << 22),
        name="finish",
    )(scal, tangent, rest)
    came[0] = after(came[0], tangent)
    for j, row in zip(range(2, n_space, 2), came):
        sens = jnp.where(source // 2 == (mine ^ j) // 2, row, sens)
    return tangent, sens.reshape(2, 1, -1)


def solution(mesh):
    return jax.shard_map(
        local,
        mesh=mesh,
        in_specs=(
            P("dir", None, "space", None, None),
            P("space", None, None),
            P("dir", "space", None),
            P(),
            P(),
        ),
        out_specs=(P("dir", None, "space", None, None), P("dir", "space", None)),
        check_vma=False,
    )
```

```python
import functools

import jax
import jax.numpy as jnp
from jax import lax
from jax.experimental import pallas as pl
from jax.experimental.pallas import tpu as pltpu
from jax.sharding import PartitionSpec as P

spread_a = 0.08
spread_b = 0.06
drift = 0.25
decay_rate = 0.05
rate_scale = 0.1

keep_a = 1.0 - 6.0 * spread_a - drift
keep_b = 1.0 - 6.0 * spread_b - drift - decay_rate
back_a = (spread_a + drift) / spread_a
back_b = (spread_b + drift) / spread_b

EDGE = 8
PAD = 8
CHUNK = 24
ANY = pl.BlockSpec(memory_space=pl.ANY)
SMEM = pl.BlockSpec(memory_space=pltpu.SMEM)
VMEM = pl.BlockSpec(memory_space=pltpu.VMEM)


def chunks(rows):
    return [(at, min(CHUNK, rows - at)) for at in range(0, rows, CHUNK)]


def run_all(copies):
    for copy in copies:
        copy.start()
    for copy in copies:
        copy.wait()


def arrange(scal, store, rate, mine, other, rate_m, sems):
    core, odd = scal[0], scal[1]
    rows = mine.shape[2]
    shift = rate.shape[1] // 2 - EDGE
    first = pl.multiple_of(core * shift, 8)
    second = pl.multiple_of((1 - core) * shift, 8)
    copies = []
    for m in range(4):
        layer = jnp.where(odd == 1, 3 - m, m)
        for start, target in ((second, other), (first, mine)):
            copies.append((store.at[0, :, layer, pl.ds(start, rows)], target.at[:, m]))
        copies.append((rate.at[layer, pl.ds(first, rows)], rate_m.at[pl.ds(rows * m, rows)]))
    run_all([pltpu.make_async_copy(a, b, sems.at[i]) for i, (a, b) in enumerate(copies)])


def exact_dot(a, b):
    return jnp.dot(a, b, precision=lax.Precision.HIGHEST, preferred_element_type=jnp.float32)


def window(scal, own, sib, out):
    half = own.shape[2] // 2
    for core in range(2):

        @pl.when(scal[0] == core)
        def _():
            at = core * (half - 1)
            for d in range(4):
                for k in range(2):
                    block = (own if d < 2 else sib)[d % 2, k, at : at + half + 1]
                    out[pl.ds((2 * d + k) * (half + 1), half + 1)] = block


def expand(scal, where, *refs):
    held, vfine, blocks = refs[:-2], refs[-2], refs[-1]
    core = scal[0]
    rows = vfine.shape[2]
    shift = rows - 2 * EDGE
    count = held[0].shape[1] // 8
    tall = blocks.shape[1]
    row = lax.broadcasted_iota(jnp.int32, (rows, 4 * tall), 0) + core * shift
    column = lax.broadcasted_iota(jnp.int32, (rows, 4 * tall), 1)
    place = column % tall
    there = 4 * (place + core * (count - 2)) + column // tall
    pick_rows = ((row // 4 == there) & (place < count)).astype(jnp.float32)
    lane = lax.broadcasted_iota(jnp.int32, (128, 512), 0)
    z = lax.broadcasted_iota(jnp.int32, (128, 512), 1)
    pick_lanes = (lane == 32 * (z // 128) + (z % 128) // 4).astype(jnp.float32)
    blocks[...] = jnp.zeros(blocks.shape, jnp.float32)
    for k in range(8):
        for d in range(4):
            block = jnp.zeros((count, 128), jnp.float32)
            for i, ref in enumerate(held):
                for j in range(2):
                    for h in range(2):
                        hit = (where[k] == 2 * i + j) & (where[8 + k] == h)
                        block = jnp.where(hit, ref[j, pl.ds((2 * d + h) * count, count)], block)
            blocks[d, pl.ds(0, count)] = block
        wide = exact_dot(blocks[...].reshape(4 * tall, 128), pick_lanes)
        table = jnp.concatenate(
            [
                jnp.concatenate(
                    [wide[tall * d : tall * (d + 1), 128 * j : 128 * (j + 1)] for j in range(4)], 0
                )
                for d in range(4)
            ],
            1,
        )
        filled = exact_dot(pick_rows, table)
        for d in range(4):
            vfine[d, k] = filled[:, 128 * d : 128 * (d + 1)]


def masks(rows):
    lane = lax.broadcasted_iota(jnp.int32, (rows, 128), 1)
    return lane == 0, lane == 127


def around(ref, lead, layer, before, after, at, rows):
    first, last = masks(rows)
    here = ref[lead, layer, pl.ds(PAD + at, rows)]
    total = ref[lead, layer, pl.ds(PAD - 1 + at, rows)] + ref[lead, layer, pl.ds(PAD + 1 + at, rows)]
    total = total + jnp.where(first, 0.0, pltpu.roll(here, 1, 1))
    total = total + jnp.where(last, 0.0, pltpu.roll(here, 127, 1))
    total = total + ref[lead, after, pl.ds(PAD + at, rows)]
    return here, total, ref[lead, before, pl.ds(PAD + at, rows)]


def clear_pads(ref):
    dirs, layers, rows, lanes = ref.shape
    zero = jnp.zeros((dirs, PAD, lanes), jnp.float32)

    @pl.loop(0, layers)
    def _(i):
        ref[:, i, pl.ds(0, PAD)] = zero
        ref[:, i, pl.ds(rows - PAD, PAD)] = zero


def clear_layer(ref, layer):
    ref[:, layer] = jnp.zeros((ref.shape[0], ref.shape[2], ref.shape[3]), jnp.float32)


def update(source, target, field_at, state_at, out_at, sigma, fields, weight, rows):
    p_ref, q_ref = source
    p_out, q_out, pad = target
    for at, n in chunks(rows):
        a = fields[0, field_at, pl.ds(at, n)]
        b = fields[1, field_at, pl.ds(at, n)]
        hold_a = keep_a - b
        hold_b = keep_b + a
        for d in range(4):
            p, p_sum, p_back = around(p_ref, d, state_at, state_at - sigma, state_at + sigma, at, n)
            q, q_sum, q_back = around(q_ref, d, state_at, state_at - sigma, state_at + sigma, at, n)
            w = weight[d, field_at, pl.ds(at, n)]
            p_out[d, out_at, pl.ds(pad + at, n)] = (
                spread_a * (p_sum + back_a * p_back) + hold_a * p - (a * q + w)
            )
            q_out[d, out_at, pl.ds(pad + at, n)] = (
                spread_b * (q_sum + back_b * q_back) + hold_b * q + (b * p + w)
            )


def first_step(
    scal, rate_m, rate_e, rate_l, s_a, s_b, e_a, e_b, l_a, l_b, far_e, far_l, v,
    state, rate, slab, far, q1, p2, q2, sems,
):
    sigma = 1 - 2 * scal[1]
    has_late = scal[2]
    p3, q3 = state.at[0], state.at[1]
    rows = rate.shape[1]
    moves = [(rate_m.at[pl.ds(rows * j, rows)], rate.at[4 + j]) for j in range(4)]
    moves += [(s_a, slab.at[:, pl.ds(4, 2)]), (s_b, slab.at[:, pl.ds(6, 2)])]
    for j in range(4):
        moves.append((rate_e.at[pl.ds(rows * j, rows)], rate.at[11 - j]))
        moves.append((rate_l.at[pl.ds(rows * j, rows)], rate.at[3 - j]))
    for j in range(2):
        moves.append((e_a.at[:, j], slab.at[:, 11 - j]))
        moves.append((e_b.at[:, j], slab.at[:, 9 - j]))
        moves.append((l_a.at[:, j], slab.at[:, 3 - j]))
        moves.append((l_b.at[:, j], slab.at[:, 1 - j]))
    moves += [(far_l, far.at[0]), (far_e, far.at[1])]
    copies = [pltpu.make_async_copy(a, b, sems.at[i]) for i, (a, b) in enumerate(moves)]
    for copy in copies:
        copy.start()
    for ref in (q1, p2, q2, p3, q3):
        clear_pads(ref)
    for ref in (p2, q2):
        clear_layer(ref, 3)
    for ref in (p3, q3):
        clear_layer(ref, 2)
    for copy in copies:
        copy.wait()

    for i, (layer, coarse) in enumerate(((0, 0), (13, 7))):
        for at, n in chunks(rows):
            w = far[i, pl.ds(at, n)]
            for d in range(4):
                q1[d, layer, pl.ds(PAD + at, n)] = w * v[d, coarse, pl.ds(at, n)]

    @pl.loop(0, 12)
    def _(i):
        coarse = (i + 2) // 2
        for at, n in chunks(rows):
            scaled = rate_scale * rate[i, pl.ds(at, n)]
            b = slab[1, i, pl.ds(at, n)]
            a = scaled * slab[0, i, pl.ds(at, n)]
            w = a * b
            slab[0, i, pl.ds(at, n)] = a
            slab[1, i, pl.ds(at, n)] = scaled * b
            for d in range(4):
                q1[d, i + 1, pl.ds(PAD + at, n)] = w * v[d, coarse, pl.ds(at, n)]

    @pl.loop(jnp.where(has_late == 1, 0, 4), 12)
    def _(i):
        for at, n in chunks(rows):
            both = slab[0, i, pl.ds(at, n)] - slab[1, i, pl.ds(at, n)]
            hold_a = both + (1.0 + keep_a)
            hold_b = both + (1.0 + keep_b)
            for d in range(4):
                q, total, back = around(q1, d, i + 1, i + 1 - sigma, i + 1 + sigma, at, n)
                p2[d, i, pl.ds(PAD + at, n)] = -(spread_a * (total + back_a * back) + hold_a * q)
                q2[d, i, pl.ds(PAD + at, n)] = spread_b * (total + back_b * back) + hold_b * q

    @pl.loop(jnp.where(has_late == 1, 0, 3), 10)
    def _(i):
        for at, n in chunks(rows):
            a = slab[0, i + 1, pl.ds(at, n)]
            b = slab[1, i + 1, pl.ds(at, n)]
            hold_a = keep_a - b
            hold_b = keep_b + a
            for d in range(4):
                p, p_sum, p_back = around(p2, d, i + 1, i + 1 - sigma, i + 1 + sigma, at, n)
                q, q_sum, q_back = around(q2, d, i + 1, i + 1 - sigma, i + 1 + sigma, at, n)
                w = q1[d, i + 2, pl.ds(PAD + at, n)]
                p3[d, i, pl.ds(PAD + at, n)] = (
                    spread_a * (p_sum + back_a * p_back) + hold_a * p - (a * q + w)
                )
                q3[d, i, pl.ds(PAD + at, n)] = (
                    spread_b * (q_sum + back_b * q_back) + hold_b * q + (b * p + w)
                )


def second_step(
    scal, rate_m, rate_e, rate_l, s_a, s_b, e_b, l_a, v, state,
    tangent, sent, means, means_sib, rate, slab, weight, p4, q4, p5, q5, p6, q6, sems, out_sems,
):
    core, odd, has_late = scal[0], scal[1], scal[2]
    sigma = 1 - 2 * odd
    rows = rate.shape[1]
    half = rows - EDGE
    p3, q3 = state.at[0], state.at[1]
    moves = [(rate_m.at[pl.ds(rows * j, rows)], rate.at[2 + j]) for j in range(4)]
    moves += [(s_a, slab.at[:, pl.ds(2, 2)]), (s_b, slab.at[:, pl.ds(4, 2)])]
    for j in range(2):
        moves.append((rate_e.at[pl.ds(rows * (3 - j), rows)], rate.at[6 + j]))
        moves.append((rate_l.at[pl.ds(rows * j, rows)], rate.at[1 - j]))
        moves.append((e_b.at[:, 1 - j], slab.at[:, 6 + j]))
        moves.append((l_a.at[:, j], slab.at[:, 1 - j]))
    copies = [pltpu.make_async_copy(a, b, sems.at[i]) for i, (a, b) in enumerate(moves)]
    for copy in copies:
        copy.start()
    for ref in (p4, q4, p5, q5):
        clear_pads(ref)
    for ref in (p4, q4):
        clear_layer(ref, 1)
    for ref in (p5, q5):
        clear_layer(ref, 0)
    for copy in copies:
        copy.wait()

    @pl.loop(0, 8)
    def _(i):
        coarse = i // 2 + 2
        for at, n in chunks(rows):
            scaled = rate_scale * rate[i, pl.ds(at, n)]
            b = slab[1, i, pl.ds(at, n)]
            a = scaled * slab[0, i, pl.ds(at, n)]
            w = a * b
            slab[0, i, pl.ds(at, n)] = a
            slab[1, i, pl.ds(at, n)] = scaled * b
            for d in range(4):
                weight[d, i, pl.ds(at, n)] = w * v[d, coarse, pl.ds(at, n)]

    @pl.loop(jnp.where(has_late == 1, 0, 2), 8)
    def _(i):
        update((p3, q3), (p4, q4, PAD), i, i + 1, i, sigma, slab, weight, rows)

    @pl.loop(jnp.where(has_late == 1, 0, 1), 6)
    def _(i):
        update((p4, q4), (p5, q5, PAD), i + 1, i + 1, i, sigma, slab, weight, rows)

    start = pl.multiple_of(core * EDGE, 8)
    place = pl.multiple_of(core * half, 8)

    def writes(i):
        layer = jnp.where(odd == 1, 3 - i, i)
        for j, ref in enumerate((p6, q6)):
            yield pltpu.make_async_copy(
                ref.at[pl.ds(0, 2), i, pl.ds(start, half)],
                tangent.at[:, j, layer, pl.ds(place, half)],
                out_sems.at[i, j],
            )
            yield pltpu.make_async_copy(
                ref.at[pl.ds(2, 2), i, pl.ds(start, half)],
                sent.at[:, j, layer],
                out_sems.at[i, 2 + j],
            )

    @pl.loop(0, 4)
    def _(i):
        update((p5, q5), (p6, q6, 0), i + 2, i + 1, i, sigma, slab, weight, rows)
        for copy in writes(i):
            copy.start()

    packed = half // 16
    row = lax.broadcasted_iota(jnp.int32, (4 * packed, half), 0)
    column = lax.broadcasted_iota(jnp.int32, (4 * packed, half), 1)
    sum_rows = (column // 4 == 4 * (row % packed) + row // packed).astype(jnp.float32)
    lane = lax.broadcasted_iota(jnp.int32, (512, 128), 1)
    z = lax.broadcasted_iota(jnp.int32, (512, 128), 0)
    sum_lanes = (lane == 32 * (z // 128) + (z % 128) // 4).astype(jnp.float32)
    pairs = [
        q6[d, 2 * k, pl.ds(start, half)] + q6[d, 2 * k + 1, pl.ds(start, half)]
        for d in range(4)
        for k in range(2)
    ]
    summed = exact_dot(sum_rows, jnp.concatenate(pairs, 1))
    spread = jnp.concatenate(
        [
            jnp.concatenate(
                [summed[packed * j : packed * (j + 1), 128 * i : 128 * (i + 1)] for j in range(4)], 1
            )
            for i in range(8)
        ],
        0,
    )
    total = exact_dot(spread, sum_lanes) * (1.0 / 32.0)
    for d in range(4):
        for k in range(2):
            layer = jnp.where(odd == 1, 1 - k, k)
            (means if d < 2 else means_sib)[d % 2, layer] = total[packed * (2 * d + k) : packed * (2 * d + k + 1)]

    @pl.loop(0, 4)
    def _(i):
        for copy in writes(i):
            copy.wait()


def finish(scal, held, received, tangent, sems):
    half = received.shape[3]
    place = pl.multiple_of((1 - scal[0]) * half, 8)
    run_all(
        [
            pltpu.make_async_copy(
                received.at[i, j], tangent.at[i, j, :, pl.ds(place, half)], sems.at[i, j]
            )
            for i in range(2)
            for j in range(2)
        ]
    )


def cost(flops, moved):
    return pl.CostEstimate(flops=flops, bytes_accessed=moved, transcendentals=0)


def after(value, *others):
    return lax.optimization_barrier((value, *others))[0]


def params(megabytes):
    return pltpu.CompilerParams(vmem_limit_bytes=megabytes << 20)


def stay(value):
    return pltpu.with_memory_space_constraint(value, pltpu.VMEM)


def vmem(*dims):
    return pltpu.VMEM(dims, jnp.float32)


def shape(*dims):
    return jax.ShapeDtypeStruct(dims, jnp.float32)


def local(store, rate, directions, owner_map, block_map):
    layers, width_y, width_z = rate.shape
    half = width_y // 2
    rows = half + EDGE
    n_space = lax.axis_size("space")
    mine = lax.axis_index("space")
    group = lax.axis_index("dir")
    core, column = group & 1, group >> 1
    odd = mine & 1
    has_late = ((mine > 0) & (mine < n_space - 1)).astype(jnp.int32)
    scal = jnp.stack([core, odd, has_late]).astype(jnp.int32)

    across_core = [(i, i ^ 1) for i in range(4)]
    across_column = [(i, i ^ 2) for i in range(4)]
    swap = [(i, i ^ 1) for i in range(n_space)]
    ahead = [(i, i + 2) for i in range(0, n_space - 2, 2)] + [(i, i - 2) for i in range(3, n_space, 2)]
    behind = [(b, a) for a, b in ahead]
    to_core = functools.partial(lax.ppermute, axis_name="dir", perm=across_core)
    to_column = functools.partial(lax.ppermute, axis_name="dir", perm=across_column)
    to_pair = functools.partial(lax.ppermute, axis_name="space", perm=swap)
    to_ahead = functools.partial(lax.ppermute, axis_name="space", perm=ahead)
    to_behind = functools.partial(lax.ppermute, axis_name="space", perm=behind)

    row = directions.reshape(2, 2, 32, 128)
    with jax.named_scope("directions_core"):
        row_sib = to_core(row)
    own, other, rate_m = pl.pallas_call(
        arrange,
        out_shape=(vmem(2, 4, rows, width_z), vmem(2, 4, rows, width_z), vmem(4 * rows, width_z)),
        in_specs=[SMEM, ANY, ANY],
        out_specs=[VMEM] * 3,
        cost_estimate=cost(0, 6 << 20),
        scratch_shapes=[pltpu.SemaphoreType.DMA((12,))],
        name="arrange",
    )(scal, store, rate)
    with jax.named_scope("store_core"):
        received = to_core(other)
    def candidates(step, received):
        here = group == owner_map[step]
        first = jnp.where(here, own[:, :2], received[:, :2])
        return first, jnp.where(here, own[:, 2:], after(received, first)[:, 2:])

    def settled(step, have, came):
        return jnp.where(column == owner_map[step] >> 1, have, came)

    have0_a, have0_b = candidates(0, received)

    coarse_own = pl.pallas_call(
        window,
        out_shape=vmem(8 * 17, 128),
        in_specs=[SMEM, VMEM, VMEM],
        out_specs=VMEM,
        name="window",
    )(scal, after(row, rate_m), row_sib)
    with jax.named_scope("directions_pair"):
        pair = jnp.stack([coarse_own, after(to_pair(coarse_own), have0_a)])
    held = [pair]
    for j in range(2, n_space, 2):
        with jax.named_scope("directions_space"):
            held.append(lax.ppermute(pair, "space", [(i, i ^ j) for i in range(n_space)]))
    have1_a, have1_b = candidates(1, after(received, have0_a, pair))
    with jax.named_scope("rate_pair"):
        rate_e = to_pair(after(rate_m, received))
    with jax.named_scope("slab0_column"):
        came0_a = to_column(have0_a)
    with jax.named_scope("slab0_column"):
        came0_b = to_column(after(have0_b, came0_a, have1_a, have1_b, *held))
    with jax.named_scope("rate_ahead"):
        rate_l = to_ahead(rate_e)

    local_coarse = jnp.arange(8, dtype=jnp.int32) - 3
    coarse_at = 2 * mine + jnp.where(odd == 1, 1 - local_coarse, local_coarse)
    block = block_map[jnp.clip(coarse_at >> 1, 0, n_space - 1)] ^ mine
    coarse_scal = jnp.concatenate([block, coarse_at & 1]).astype(jnp.int32)
    s0_a = settled(0, have0_a, came0_a)
    with jax.named_scope("slab0_pair"):
        e0_a = to_pair(after(s0_a, rate_e))
    s0_b = settled(0, have0_b, came0_b)
    w_near = rate_scale * rate_m[:rows] * s0_a[0, 0] * s0_a[1, 0]
    w_late = rate_scale * rate_m[3 * rows : 4 * rows] * s0_b[0, 1] * s0_b[1, 1]
    with jax.named_scope("far_layers"):
        far_e = to_behind(w_near)
        far_l = to_ahead(w_late)
    with jax.named_scope("slab0_pair"):
        e0_b = to_pair(after(s0_b, e0_a))
    vfine = pl.pallas_call(
        expand,
        out_shape=vmem(4, 8, rows, width_z),
        in_specs=[SMEM, SMEM] + [VMEM] * len(held),
        out_specs=VMEM,
        scratch_shapes=[vmem(4, 24, 128)],
        name="expand",
        cost_estimate=cost(0, 25 << 20),
        compiler_params=params(16),
    )(scal, coarse_scal, *held)
    with jax.named_scope("slab1_column"):
        came1_a = to_column(after(have1_a, e0_a))
        came1_b = to_column(after(have1_b, e0_b, far_e, far_l))
    with jax.named_scope("slab0_ahead"):
        l0_a = to_ahead(after(e0_a, s0_b, rate_l))
        l0_b = to_ahead(after(e0_b, l0_a, far_e, far_l, vfine))
    s1_a = settled(1, have1_a, came1_a)
    with jax.named_scope("slab1_pair"):
        e1_a = to_pair(after(s1_a, e0_b))
    with jax.named_scope("slab1_ahead"):
        l1_a = to_ahead(after(e1_a, l0_b))
    s1_b = settled(1, have1_b, came1_b)
    with jax.named_scope("slab1_pair"):
        e1_b = to_pair(after(s1_b, e1_a))
    l0_b = after(l0_b, s1_b, e1_a)

    tall = rows + 2 * PAD
    state = pl.pallas_call(
        first_step,
        out_shape=vmem(2, 4, 10, tall, width_z),
        in_specs=[SMEM] + [ANY] * 11 + [VMEM],
        out_specs=VMEM,
        scratch_shapes=[
            vmem(12, rows, width_z),
            vmem(2, 12, rows, width_z),
            vmem(2, rows, width_z),
            vmem(4, 14, tall, width_z),
            vmem(4, 12, tall, width_z),
            vmem(4, 12, tall, width_z),
            pltpu.SemaphoreType.DMA((24,)),
        ],
        name="first_step",
        cost_estimate=cost(0, 50 << 20),
        compiler_params=params(31),
    )(scal, rate_m, rate_e, rate_l, s0_a, s0_b, e0_a, e0_b, l0_a, l0_b, far_e, far_l, stay(vfine))

    tangent, sent, first, second = pl.pallas_call(
        second_step,
        out_shape=(
            shape(2, 2, 4, width_y, width_z),
            shape(2, 2, 4, half, width_z),
            vmem(2, 2, half // 16, 128),
            vmem(2, 2, half // 16, 128),
        ),
        in_specs=[SMEM] + [ANY] * 7 + [VMEM] * 2,
        out_specs=[ANY, ANY, VMEM, VMEM],
        scratch_shapes=[
            vmem(8, rows, width_z),
            vmem(2, 8, rows, width_z),
            vmem(4, 8, rows, width_z),
            vmem(4, 8, tall, width_z),
            vmem(4, 8, tall, width_z),
            vmem(4, 6, tall, width_z),
            vmem(4, 6, tall, width_z),
            vmem(4, 4, rows, width_z),
            vmem(4, 4, rows, width_z),
            pltpu.SemaphoreType.DMA((14,)),
            pltpu.SemaphoreType.DMA((4, 4)),
        ],
        name="second_step",
        cost_estimate=cost(0, 55 << 20),
        compiler_params=params(36),
    )(scal, rate_m, rate_e, rate_l, s1_a, s1_b, e1_b, l1_a, stay(vfine), stay(state))


    def joined(a, b):
        return jnp.where(core == 0, jnp.concatenate([a, b], 2), jnp.concatenate([b, a], 2))

    both = [(i * n_space + j, (i ^ 1) * n_space + (j ^ 1)) for i in range(4) for j in range(n_space)]
    with jax.named_scope("means_near"):
        here = joined(first, to_core(second))
        there = joined(to_pair(first), lax.ppermute(second, ("dir", "space"), both))
    with jax.named_scope("tangent_core"):
        rest = to_core(after(sent, here, there))
    source = jnp.sum(jnp.where(block_map == mine, jnp.arange(n_space, dtype=jnp.int32), 0))
    sens = jnp.where(source == mine, here, there)
    came = []
    for j in range(2, n_space, 2):
        row = jnp.where(block_map[mine] == mine ^ j, here, there)
        pairs = [(i, i ^ j) for i in range(n_space)]
        with jax.named_scope("means_space"):
            came.append(lax.ppermute(row, "space", pairs))
    tangent = pl.pallas_call(
        finish,
        out_shape=shape(2, 2, 4, width_y, width_z),
        in_specs=[SMEM, ANY, VMEM],
        out_specs=ANY,
        scratch_shapes=[pltpu.SemaphoreType.DMA((2, 2))],
        input_output_aliases={1: 0},
        cost_estimate=cost(0, 2 << 22),
        name="finish",
    )(scal, tangent, rest)
    came[0] = after(came[0], tangent)
    for j, row in zip(range(2, n_space, 2), came):
        sens = jnp.where(source >> 1 == (mine ^ j) >> 1, row, sens)
    return tangent, sens.reshape(2, 1, -1)


def solution(mesh):
    return jax.shard_map(
        local,
        mesh=mesh,
        in_specs=(
            P("dir", None, "space", None, None),
            P("space", None, None),
            P("dir", "space", None),
            P(),
            P(),
        ),
        out_specs=(P("dir", None, "space", None, None), P("dir", "space", None)),
        check_vma=False,
    )
```

```python
import functools

import jax
import jax.numpy as jnp
from jax import lax
from jax.experimental import pallas as pl
from jax.experimental.pallas import tpu as pltpu
from jax.sharding import PartitionSpec as P

spread_a = 0.08
spread_b = 0.06
drift = 0.25
decay_rate = 0.05
rate_scale = 0.1

keep_a = 1.0 - 6.0 * spread_a - drift
keep_b = 1.0 - 6.0 * spread_b - drift - decay_rate
back_a = (spread_a + drift) / spread_a
back_b = (spread_b + drift) / spread_b

EDGE = 8
PAD = 8
CHUNK = 24
ANY = pl.BlockSpec(memory_space=pl.ANY)
SMEM = pl.BlockSpec(memory_space=pltpu.SMEM)
VMEM = pl.BlockSpec(memory_space=pltpu.VMEM)


def chunks(rows):
    return [(at, min(CHUNK, rows - at)) for at in range(0, rows, CHUNK)]


def run_all(copies):
    for copy in copies:
        copy.start()
    for copy in copies:
        copy.wait()


def arrange(scal, store, rate, mine, other, rate_m, sems):
    core, odd = scal[0], scal[1]
    rows = mine.shape[2]
    shift = rate.shape[1] // 2 - EDGE
    first = pl.multiple_of(core * shift, 8)
    second = pl.multiple_of((1 - core) * shift, 8)
    copies = []
    for m in range(4):
        layer = jnp.where(odd == 1, 3 - m, m)
        for start, target in ((second, other), (first, mine)):
            copies.append((store.at[0, :, layer, pl.ds(start, rows)], target.at[:, m]))
        copies.append((rate.at[layer, pl.ds(first, rows)], rate_m.at[pl.ds(rows * m, rows)]))
    run_all([pltpu.make_async_copy(a, b, sems.at[i]) for i, (a, b) in enumerate(copies)])


def parts(value):
    first = value.astype(jnp.bfloat16)
    rest = value - first.astype(jnp.float32)
    second = rest.astype(jnp.bfloat16)
    return [first, second, (rest - second.astype(jnp.float32)).astype(jnp.bfloat16)]


def exact_dot(a, b):
    return jnp.dot(a, b, precision=lax.Precision.HIGHEST, preferred_element_type=jnp.float32)


def window(scal, own, sib, out):
    half = own.shape[2] // 2
    for core in range(2):

        @pl.when(scal[0] == core)
        def _():
            at = core * (half - 1)
            for d in range(4):
                for k in range(2):
                    block = (own if d < 2 else sib)[d % 2, k, at : at + half + 1]
                    out[pl.ds((2 * d + k) * (half + 1), half + 1)] = block


def expand(scal, where, *refs):
    held, vfine, blocks = refs[:-2], refs[-2], refs[-1]
    core = scal[0]
    rows = vfine.shape[2]
    shift = rows - 2 * EDGE
    count = held[0].shape[1] // 8
    tall = blocks.shape[1]
    padded = (rows + 15) // 16 * 16
    row = lax.broadcasted_iota(jnp.int32, (padded, 4 * tall), 0) + core * shift
    column = lax.broadcasted_iota(jnp.int32, (padded, 4 * tall), 1)
    place = column % tall
    there = 4 * (place + core * (count - 2)) + column // tall
    pick_rows = ((row // 4 == there) & (place < count)).astype(jnp.float32)
    pick_rows = jnp.concatenate([pick_rows] * 3, 1).astype(jnp.bfloat16)
    lane = lax.broadcasted_iota(jnp.int32, (128, 512), 0)
    z = lax.broadcasted_iota(jnp.int32, (128, 512), 1)
    pick_lanes = (lane == 32 * (z // 128) + (z % 128) // 4).astype(jnp.float32)
    pick_lanes = jnp.concatenate([pick_lanes] * 3, 0).astype(jnp.bfloat16)
    blocks[...] = jnp.zeros(blocks.shape, jnp.float32)
    for k in range(8):
        for d in range(4):
            block = jnp.zeros((count, 128), jnp.float32)
            for i, ref in enumerate(held):
                for j in range(2):
                    for h in range(2):
                        hit = (where[k] == 2 * i + j) & (where[8 + k] == h)
                        block = jnp.where(hit, ref[j, pl.ds((2 * d + h) * count, count)], block)
            blocks[d, pl.ds(0, count)] = block
        wide = jnp.dot(
            jnp.concatenate(parts(blocks[...].reshape(4 * tall, 128)), 1),
            pick_lanes,
            preferred_element_type=jnp.float32,
        )
        table = jnp.concatenate(
            [
                jnp.concatenate(
                    [wide[tall * d : tall * (d + 1), 128 * j : 128 * (j + 1)] for j in range(4)], 0
                )
                for d in range(4)
            ],
            1,
        )
        filled = jnp.dot(
            pick_rows, jnp.concatenate(parts(table), 0), preferred_element_type=jnp.float32
        )[:rows]
        for d in range(4):
            vfine[d, k] = filled[:, 128 * d : 128 * (d + 1)]


def masks(rows):
    lane = lax.broadcasted_iota(jnp.int32, (rows, 128), 1)
    return lane == 0, lane == 127


def around(ref, lead, layer, before, after, at, rows):
    first, last = masks(rows)
    here = ref[lead, layer, pl.ds(PAD + at, rows)]
    total = ref[lead, layer, pl.ds(PAD - 1 + at, rows)] + ref[lead, layer, pl.ds(PAD + 1 + at, rows)]
    total = total + jnp.where(first, 0.0, pltpu.roll(here, 1, 1))
    total = total + jnp.where(last, 0.0, pltpu.roll(here, 127, 1))
    total = total + ref[lead, after, pl.ds(PAD + at, rows)]
    return here, total, ref[lead, before, pl.ds(PAD + at, rows)]


def clear_pads(ref, layers=None):
    dirs, every, rows, lanes = ref.shape
    zero = jnp.zeros((dirs, PAD, lanes), jnp.float32)

    @pl.loop(0, layers or every)
    def _(i):
        ref[:, i, pl.ds(0, PAD)] = zero
        ref[:, i, pl.ds(rows - PAD, PAD)] = zero


def clear_layer(ref, layer):
    ref[:, layer] = jnp.zeros((ref.shape[0], ref.shape[2], ref.shape[3]), jnp.float32)


def update(source, target, field_at, state_at, out_at, sigma, fields, weight, rows):
    p_ref, q_ref = source
    p_out, q_out, pad = target
    for at, n in chunks(rows):
        a = fields[0, field_at, pl.ds(at, n)]
        b = fields[1, field_at, pl.ds(at, n)]
        hold_a = keep_a - b
        hold_b = keep_b + a
        for d in range(4):
            p, p_sum, p_back = around(p_ref, d, state_at, state_at - sigma, state_at + sigma, at, n)
            q, q_sum, q_back = around(q_ref, d, state_at, state_at - sigma, state_at + sigma, at, n)
            w = weight[d, field_at, pl.ds(at, n)]
            p_out[d, out_at, pl.ds(pad + at, n)] = (
                spread_a * (p_sum + back_a * p_back) + hold_a * p - (a * q + w)
            )
            q_out[d, out_at, pl.ds(pad + at, n)] = (
                spread_b * (q_sum + back_b * q_back) + hold_b * q + (b * p + w)
            )


def weigh(low, high, rate, slab, v, q1):
    rows = rate.shape[1]

    @pl.loop(low, high)
    def _(i):
        coarse = (i + 2) // 2
        for at, n in chunks(rows):
            scaled = rate_scale * rate[i, pl.ds(at, n)]
            b = slab[1, i, pl.ds(at, n)]
            a = scaled * slab[0, i, pl.ds(at, n)]
            w = a * b
            slab[0, i, pl.ds(at, n)] = a
            slab[1, i, pl.ds(at, n)] = scaled * b
            for d in range(4):
                q1[d, i + 1, pl.ds(PAD + at, n)] = w * v[d, coarse, pl.ds(at, n)]


def outermost(far, layer, coarse, v, q1):
    for at, n in chunks(far.shape[0]):
        w = far[pl.ds(at, n)]
        for d in range(4):
            q1[d, layer, pl.ds(PAD + at, n)] = w * v[d, coarse, pl.ds(at, n)]


def second_update(low, high, sigma, slab, q1, p2, q2):
    rows = slab.shape[2]

    @pl.loop(low, high)
    def _(i):
        for at, n in chunks(rows):
            both = slab[0, i, pl.ds(at, n)] - slab[1, i, pl.ds(at, n)]
            hold_a = both + (1.0 + keep_a)
            hold_b = both + (1.0 + keep_b)
            for d in range(4):
                q, total, back = around(q1, d, i + 1, i + 1 - sigma, i + 1 + sigma, at, n)
                p2[d, i, pl.ds(PAD + at, n)] = -(spread_a * (total + back_a * back) + hold_a * q)
                q2[d, i, pl.ds(PAD + at, n)] = spread_b * (total + back_b * back) + hold_b * q


def third_update(low, high, sigma, slab, q1, p2, q2, p3, q3, shift):
    rows = slab.shape[2]

    @pl.loop(low, high)
    def _(i):
        for at, n in chunks(rows):
            a = slab[0, i + 1, pl.ds(at, n)]
            b = slab[1, i + 1, pl.ds(at, n)]
            hold_a = keep_a - b
            hold_b = keep_b + a
            for d in range(4):
                p, p_sum, p_back = around(p2, d, i + 1, i + 1 - sigma, i + 1 + sigma, at, n)
                q, q_sum, q_back = around(q2, d, i + 1, i + 1 - sigma, i + 1 + sigma, at, n)
                w = q1[d, i + 2, pl.ds(PAD + at, n)]
                p3[d, i - shift, pl.ds(PAD + at, n)] = (
                    spread_a * (p_sum + back_a * p_back) + hold_a * p - (a * q + w)
                )
                q3[d, i - shift, pl.ds(PAD + at, n)] = (
                    spread_b * (q_sum + back_b * q_back) + hold_b * q + (b * p + w)
                )


def first_step(
    scal, rate_m, rate_e, rate_l, s_a, s_b, e_a, e_b, l_a, far_e, v,
    state, edge1, edge2, edge_slab, rate, slab, far, q1, p2, q2, sems,
):
    sigma = 1 - 2 * scal[1]
    has_late = scal[2]
    p3, q3 = state.at[0], state.at[1]
    rows = rate.shape[1]
    moves = [(rate_m.at[pl.ds(rows * j, rows)], rate.at[4 + j]) for j in range(4)]
    moves += [(s_a, slab.at[:, pl.ds(4, 2)]), (s_b, slab.at[:, pl.ds(6, 2)])]
    for j in range(4):
        moves.append((rate_e.at[pl.ds(rows * j, rows)], rate.at[11 - j]))
    for j in range(2):
        moves.append((rate_l.at[pl.ds(rows * j, rows)], rate.at[3 - j]))
        moves.append((e_a.at[:, j], slab.at[:, 11 - j]))
        moves.append((e_b.at[:, j], slab.at[:, 9 - j]))
        moves.append((l_a.at[:, j], slab.at[:, 3 - j]))
    moves.append((far_e, far))
    copies = [pltpu.make_async_copy(a, b, sems.at[i]) for i, (a, b) in enumerate(moves)]
    for copy in copies:
        copy.start()
    for ref in (q1, p2, q2, p3, q3):
        clear_pads(ref)

    @pl.when(has_late == 0)
    def _():
        for ref in (p2, q2):
            clear_layer(ref, 3)

    for copy in copies:
        copy.wait()
    outermost(far, 13, 7, v, q1)
    weigh(2, 12, rate, slab, v, q1)
    second_update(jnp.where(has_late == 1, 3, 4), 12, sigma, slab, q1, p2, q2)
    moves = [(q1.at[:, pl.ds(3, 2)], edge1), (slab.at[:, pl.ds(2, 2)], edge_slab)]
    moves += [(p2.at[:, pl.ds(3, 2)], edge2.at[0]), (q2.at[:, pl.ds(3, 2)], edge2.at[1])]
    copies = [pltpu.make_async_copy(a, b, sems.at[i]) for i, (a, b) in enumerate(moves)]
    for copy in copies:
        copy.start()
    third_update(3, 10, sigma, slab, q1, p2, q2, p3, q3, 3)
    for copy in copies:
        copy.wait()


def late_layers(
    scal, rate_l, l_b, far_l, v, state, edge1, edge2, edge_slab,
    late, rate, slab, far, q1, p2, q2, sems,
):
    sigma = 1 - 2 * scal[1]
    rows = rate.shape[1]
    p3, q3 = late.at[0], late.at[1]
    kept = [
        pltpu.make_async_copy(state.at[i, :, pl.ds(0, 2)], late.at[i, :, pl.ds(3, 2)], sems.at[i])
        for i in range(2)
    ]
    for copy in kept:
        copy.start()

    @pl.when(scal[2] == 0)
    def _():
        for ref in (p3, q3):
            clear_layer(ref, 2)

    @pl.when(scal[2] == 1)
    def _():
        moves = [(far_l, far), (edge1, q1.at[:, pl.ds(3, 2)]), (edge_slab, slab.at[:, pl.ds(2, 2)])]
        moves += [(edge2.at[0], p2.at[:, pl.ds(3, 2)]), (edge2.at[1], q2.at[:, pl.ds(3, 2)])]
        for j in range(2):
            moves.append((rate_l.at[pl.ds(rows * (2 + j), rows)], rate.at[1 - j]))
            moves.append((l_b.at[:, j], slab.at[:, 1 - j]))
        copies = [pltpu.make_async_copy(a, b, sems.at[2 + i]) for i, (a, b) in enumerate(moves)]
        for copy in copies:
            copy.start()
        for ref in (q1, p2, q2, p3, q3):
            clear_pads(ref, 3)
        for copy in copies:
            copy.wait()
        outermost(far, 0, 0, v, q1)
        weigh(0, 2, rate, slab, v, q1)
        second_update(0, 3, sigma, slab, q1, p2, q2)
        third_update(0, 3, sigma, slab, q1, p2, q2, p3, q3, 0)

    for copy in kept:
        copy.wait()


def second_step(
    scal, rate_m, rate_e, rate_l, s_a, s_b, e_b, l_a, v, state, late,
    tangent, sent, means, means_sib, rate, slab, weight, p4, q4, p5, q5, p6, q6, sems, out_sems,
):
    core, odd, has_late = scal[0], scal[1], scal[2]
    sigma = 1 - 2 * odd
    rows = rate.shape[1]
    half = rows - EDGE
    moves = [(rate_m.at[pl.ds(rows * j, rows)], rate.at[2 + j]) for j in range(4)]
    moves += [(s_a, slab.at[:, pl.ds(2, 2)]), (s_b, slab.at[:, pl.ds(4, 2)])]
    for j in range(2):
        moves.append((rate_e.at[pl.ds(rows * (3 - j), rows)], rate.at[6 + j]))
        moves.append((rate_l.at[pl.ds(rows * j, rows)], rate.at[1 - j]))
        moves.append((e_b.at[:, 1 - j], slab.at[:, 6 + j]))
        moves.append((l_a.at[:, j], slab.at[:, 1 - j]))
    copies = [pltpu.make_async_copy(a, b, sems.at[i]) for i, (a, b) in enumerate(moves)]
    for copy in copies:
        copy.start()
    for ref in (p4, q4, p5, q5):
        clear_pads(ref)

    @pl.when(has_late == 0)
    def _():
        for ref, layer in ((p4, 1), (q4, 1), (p5, 0), (q5, 0)):
            clear_layer(ref, layer)

    for copy in copies:
        copy.wait()

    @pl.loop(0, 8)
    def _(i):
        coarse = i // 2 + 2
        for at, n in chunks(rows):
            scaled = rate_scale * rate[i, pl.ds(at, n)]
            b = slab[1, i, pl.ds(at, n)]
            a = scaled * slab[0, i, pl.ds(at, n)]
            w = a * b
            slab[0, i, pl.ds(at, n)] = a
            slab[1, i, pl.ds(at, n)] = scaled * b
            for d in range(4):
                weight[d, i, pl.ds(at, n)] = w * v[d, coarse, pl.ds(at, n)]

    @pl.loop(jnp.where(has_late == 1, 0, 2), 3)
    def _(i):
        update((late.at[0], late.at[1]), (p4, q4, PAD), i, i + 1, i, sigma, slab, weight, rows)

    @pl.loop(3, 8)
    def _(i):
        update((state.at[0], state.at[1]), (p4, q4, PAD), i, i - 2, i, sigma, slab, weight, rows)

    @pl.loop(jnp.where(has_late == 1, 0, 1), 6)
    def _(i):
        update((p4, q4), (p5, q5, PAD), i + 1, i + 1, i, sigma, slab, weight, rows)

    start = pl.multiple_of(core * EDGE, 8)
    place = pl.multiple_of(core * half, 8)

    def writes(i):
        layer = jnp.where(odd == 1, 3 - i, i)
        for j, ref in enumerate((p6, q6)):
            yield pltpu.make_async_copy(
                ref.at[pl.ds(0, 2), i, pl.ds(start, half)],
                tangent.at[:, j, layer, pl.ds(place, half)],
                out_sems.at[i, j],
            )
            yield pltpu.make_async_copy(
                ref.at[pl.ds(2, 2), i, pl.ds(start, half)],
                sent.at[:, j, layer],
                out_sems.at[i, 2 + j],
            )

    @pl.loop(0, 4)
    def _(i):
        update((p5, q5), (p6, q6, 0), i + 2, i + 1, i, sigma, slab, weight, rows)
        for copy in writes(i):
            copy.start()

    packed = half // 16
    row = lax.broadcasted_iota(jnp.int32, (4 * packed, half), 0)
    column = lax.broadcasted_iota(jnp.int32, (4 * packed, half), 1)
    sum_rows = (column // 4 == 4 * (row % packed) + row // packed).astype(jnp.float32)
    lane = lax.broadcasted_iota(jnp.int32, (512, 128), 1)
    z = lax.broadcasted_iota(jnp.int32, (512, 128), 0)
    sum_lanes = (lane == 32 * (z // 128) + (z % 128) // 4).astype(jnp.float32)
    pairs = [
        q6[d, 2 * k, pl.ds(start, half)] + q6[d, 2 * k + 1, pl.ds(start, half)]
        for d in range(4)
        for k in range(2)
    ]
    summed = exact_dot(sum_rows, jnp.concatenate(pairs, 1))
    spread = jnp.concatenate(
        [
            jnp.concatenate(
                [summed[packed * j : packed * (j + 1), 128 * i : 128 * (i + 1)] for j in range(4)], 1
            )
            for i in range(8)
        ],
        0,
    )
    total = exact_dot(spread, sum_lanes) * (1.0 / 32.0)
    for d in range(4):
        for k in range(2):
            layer = jnp.where(odd == 1, 1 - k, k)
            (means if d < 2 else means_sib)[d % 2, layer] = total[packed * (2 * d + k) : packed * (2 * d + k + 1)]

    @pl.loop(0, 4)
    def _(i):
        for copy in writes(i):
            copy.wait()


def finish(scal, held, received, tangent, sems):
    half = received.shape[3]
    place = pl.multiple_of((1 - scal[0]) * half, 8)
    run_all(
        [
            pltpu.make_async_copy(
                received.at[i, j], tangent.at[i, j, :, pl.ds(place, half)], sems.at[i, j]
            )
            for i in range(2)
            for j in range(2)
        ]
    )


def cost(flops, moved):
    return pl.CostEstimate(flops=flops, bytes_accessed=moved, transcendentals=0)


def after(value, *others):
    return lax.optimization_barrier((value, *others))[0]


def params(megabytes):
    return pltpu.CompilerParams(vmem_limit_bytes=megabytes << 20)


def stay(value):
    return pltpu.with_memory_space_constraint(value, pltpu.VMEM)


def vmem(*dims):
    return pltpu.VMEM(dims, jnp.float32)


def shape(*dims):
    return jax.ShapeDtypeStruct(dims, jnp.float32)


def local(store, rate, directions, owner_map, block_map):
    layers, width_y, width_z = rate.shape
    half = width_y // 2
    rows = half + EDGE
    n_space = lax.axis_size("space")
    mine = lax.axis_index("space")
    group = lax.axis_index("dir")
    core, column = group & 1, group >> 1
    odd = mine & 1
    has_late = ((mine > 0) & (mine < n_space - 1)).astype(jnp.int32)
    scal = jnp.stack([core, odd, has_late]).astype(jnp.int32)

    across_core = [(i, i ^ 1) for i in range(4)]
    across_column = [(i, i ^ 2) for i in range(4)]
    swap = [(i, i ^ 1) for i in range(n_space)]
    ahead = [(i, i + 2) for i in range(0, n_space - 2, 2)] + [(i, i - 2) for i in range(3, n_space, 2)]
    behind = [(b, a) for a, b in ahead]
    to_core = functools.partial(lax.ppermute, axis_name="dir", perm=across_core)
    to_column = functools.partial(lax.ppermute, axis_name="dir", perm=across_column)
    to_pair = functools.partial(lax.ppermute, axis_name="space", perm=swap)
    to_ahead = functools.partial(lax.ppermute, axis_name="space", perm=ahead)
    to_behind = functools.partial(lax.ppermute, axis_name="space", perm=behind)

    row = directions.reshape(2, 2, 32, 128)
    with jax.named_scope("directions_core"):
        row_sib = to_core(row)
    own, other, rate_m = pl.pallas_call(
        arrange,
        out_shape=(vmem(2, 4, rows, width_z), vmem(2, 4, rows, width_z), vmem(4 * rows, width_z)),
        in_specs=[SMEM, ANY, ANY],
        out_specs=[VMEM] * 3,
        cost_estimate=cost(0, 6 << 20),
        scratch_shapes=[pltpu.SemaphoreType.DMA((12,))],
        name="arrange",
    )(scal, store, rate)
    with jax.named_scope("store_core"):
        received = to_core(other)

    def candidates(step, received):
        here = group == owner_map[step]
        first = jnp.where(here, own[:, :2], received[:, :2])
        return first, jnp.where(here, own[:, 2:], after(received, first)[:, 2:])

    def settled(step, have, came):
        return jnp.where(column == owner_map[step] >> 1, have, came)

    have0_a, have0_b = candidates(0, received)
    have1_a, have1_b = candidates(1, after(received, have0_a))

    coarse_own = pl.pallas_call(
        window,
        out_shape=vmem(8 * 17, 128),
        in_specs=[SMEM, VMEM, VMEM],
        out_specs=VMEM,
        name="window",
    )(scal, after(row, rate_m), row_sib)
    with jax.named_scope("directions_pair"):
        pair = jnp.stack([coarse_own, after(to_pair(coarse_own), have0_b)])
    held = [pair]
    for j in range(2, n_space, 2):
        with jax.named_scope("directions_space"):
            held.append(lax.ppermute(after(pair), "space", [(i, i ^ j) for i in range(n_space)]))
    with jax.named_scope("rate_pair"):
        rate_e = to_pair(after(rate_m, received))
    with jax.named_scope("slab0_column"):
        came0_a = to_column(after(have0_a))
        came0_b = to_column(after(have0_b, came0_a, have1_a, have1_b))
    with jax.named_scope("rate_ahead"):
        rate_l = to_ahead(after(rate_e))
    s0_a = settled(0, have0_a, came0_a)
    with jax.named_scope("slab0_pair"):
        e0_a = to_pair(after(s0_a, rate_e, *held))
    s0_b = settled(0, have0_b, after(came0_b))
    w_near = rate_scale * rate_m[:rows] * s0_a[0, 0] * s0_a[1, 0]
    w_late = rate_scale * rate_m[3 * rows : 4 * rows] * s0_b[0, 1] * s0_b[1, 1]
    with jax.named_scope("far_layers"):
        far_e = to_behind(after(w_near, rate_l))
        far_l = to_ahead(after(w_late, rate_l))
    with jax.named_scope("slab1_column"):
        came1_a = to_column(after(have1_a, e0_a))
    local_coarse = jnp.arange(8, dtype=jnp.int32) - 3
    coarse_at = 2 * mine + jnp.where(odd == 1, 1 - local_coarse, local_coarse)
    block = block_map[jnp.clip(coarse_at >> 1, 0, n_space - 1)] ^ mine
    coarse_scal = jnp.concatenate([block, coarse_at & 1]).astype(jnp.int32)
    vfine = pl.pallas_call(
        expand,
        out_shape=vmem(4, 8, rows, width_z),
        in_specs=[SMEM, SMEM] + [VMEM] * len(held),
        out_specs=VMEM,
        scratch_shapes=[vmem(4, 24, 128)],
        name="expand",
        cost_estimate=cost(0, 25 << 20),
        compiler_params=params(16),
    )(scal, coarse_scal, *held[:-1], after(held[-1]))
    with jax.named_scope("slab0_pair"):
        e0_b = to_pair(after(s0_b, e0_a))
    with jax.named_scope("slab1_column"):
        came1_b = to_column(after(have1_b, e0_b, far_e, far_l))
    with jax.named_scope("slab0_ahead"):
        l0_a = to_ahead(after(e0_a, s0_b))
        l0_b = to_ahead(after(e0_b, l0_a, far_e, far_l, vfine))
    s1_a = settled(1, have1_a, came1_a)
    with jax.named_scope("slab1_pair"):
        e1_a = to_pair(after(s1_a, e0_b))
    with jax.named_scope("slab1_ahead"):
        l1_a = to_ahead(after(e1_a, l0_b))
    tall = rows + 2 * PAD
    state, *edges = pl.pallas_call(
        first_step,
        out_shape=(
            vmem(2, 4, 7, tall, width_z),
            vmem(4, 2, tall, width_z),
            vmem(2, 4, 2, tall, width_z),
            vmem(2, 2, rows, width_z),
        ),
        in_specs=[SMEM] + [ANY] * 9 + [VMEM],
        out_specs=[VMEM] * 4,
        scratch_shapes=[
            vmem(12, rows, width_z),
            vmem(2, 12, rows, width_z),
            vmem(rows, width_z),
            vmem(4, 14, tall, width_z),
            vmem(4, 12, tall, width_z),
            vmem(4, 12, tall, width_z),
            pltpu.SemaphoreType.DMA((19,)),
        ],
        name="first_step",
        cost_estimate=cost(0, 40 << 20),
        compiler_params=params(30),
    )(scal, rate_m, rate_e, rate_l, s0_a, s0_b, e0_a, e0_b, after(l0_a), far_e, stay(vfine))
    s1_b = settled(1, have1_b, after(came1_b, state))
    with jax.named_scope("slab1_pair"):
        e1_b = to_pair(after(s1_b))

    l0_b = after(l0_b, e1_a, s1_b)

    late = pl.pallas_call(
        late_layers,
        out_shape=vmem(2, 4, 5, tall, width_z),
        in_specs=[SMEM] + [ANY] * 3 + [VMEM] * 5,
        out_specs=VMEM,
        scratch_shapes=[
            vmem(2, rows, width_z),
            vmem(2, 4, rows, width_z),
            vmem(rows, width_z),
            vmem(4, 5, tall, width_z),
            vmem(4, 5, tall, width_z),
            vmem(4, 5, tall, width_z),
            pltpu.SemaphoreType.DMA((11,)),
        ],
        name="late_layers",
        cost_estimate=cost(0, 20 << 20),
        compiler_params=params(12),
    )(scal, rate_l, l0_b, far_l, stay(vfine), stay(state), *[stay(x) for x in edges])

    tangent, sent, first, second = pl.pallas_call(
        second_step,
        out_shape=(
            shape(2, 2, 4, width_y, width_z),
            shape(2, 2, 4, half, width_z),
            vmem(2, 2, half // 16, 128),
            vmem(2, 2, half // 16, 128),
        ),
        in_specs=[SMEM] + [ANY] * 7 + [VMEM] * 3,
        out_specs=[ANY, ANY, VMEM, VMEM],
        scratch_shapes=[
            vmem(8, rows, width_z),
            vmem(2, 8, rows, width_z),
            vmem(4, 8, rows, width_z),
            vmem(4, 8, tall, width_z),
            vmem(4, 8, tall, width_z),
            vmem(4, 6, tall, width_z),
            vmem(4, 6, tall, width_z),
            vmem(4, 4, rows, width_z),
            vmem(4, 4, rows, width_z),
            pltpu.SemaphoreType.DMA((14,)),
            pltpu.SemaphoreType.DMA((4, 4)),
        ],
        name="second_step",
        cost_estimate=cost(0, 55 << 20),
        compiler_params=params(36),
    )(scal, rate_m, rate_e, rate_l, s1_a, s1_b, e1_b, l1_a, stay(vfine), stay(state), stay(late))


    def joined(a, b):
        return jnp.where(core == 0, jnp.concatenate([a, b], 2), jnp.concatenate([b, a], 2))

    both = [(i * n_space + j, (i ^ 1) * n_space + (j ^ 1)) for i in range(4) for j in range(n_space)]
    with jax.named_scope("means_near"):
        here = joined(first, to_core(second))
        there = joined(to_pair(first), lax.ppermute(second, ("dir", "space"), both))
    with jax.named_scope("tangent_core"):
        rest = to_core(sent)
    source = jnp.sum(jnp.where(block_map == mine, jnp.arange(n_space, dtype=jnp.int32), 0))
    sens = jnp.where(source == mine, here, there)
    came = []
    for j in range(2, n_space, 2):
        row = jnp.where(block_map[mine] == mine ^ j, here, there)
        pairs = [(i, i ^ j) for i in range(n_space)]
        with jax.named_scope("means_space"):
            came.append(lax.ppermute(row, "space", pairs))
    tangent = pl.pallas_call(
        finish,
        out_shape=shape(2, 2, 4, width_y, width_z),
        in_specs=[SMEM, ANY, VMEM],
        out_specs=ANY,
        scratch_shapes=[pltpu.SemaphoreType.DMA((2, 2))],
        input_output_aliases={1: 0},
        cost_estimate=cost(0, 2 << 22),
        name="finish",
    )(scal, tangent, rest)
    came[0] = after(came[0], tangent)
    for j, row in zip(range(2, n_space, 2), came):
        sens = jnp.where(source >> 1 == (mine ^ j) >> 1, row, sens)
    return tangent, sens.reshape(2, 1, -1)


def solution(mesh):
    return jax.shard_map(
        local,
        mesh=mesh,
        in_specs=(
            P("dir", None, "space", None, None),
            P("space", None, None),
            P("dir", "space", None),
            P(),
            P(),
        ),
        out_specs=(P("dir", None, "space", None, None), P("dir", "space", None)),
        check_vma=False,
    )
```

```python
import functools

import jax
import jax.numpy as jnp
from jax import lax
from jax.experimental import pallas as pl
from jax.experimental.pallas import tpu as pltpu
from jax.sharding import PartitionSpec as P

spread_a = 0.08
spread_b = 0.06
drift = 0.25
decay_rate = 0.05
rate_scale = 0.1

keep_a = 1.0 - 6.0 * spread_a - drift
keep_b = 1.0 - 6.0 * spread_b - drift - decay_rate
back_a = (spread_a + drift) / spread_a
back_b = (spread_b + drift) / spread_b

EDGE = 8
PAD = 8
CHUNK = 24
ANY = pl.BlockSpec(memory_space=pl.ANY)
SMEM = pl.BlockSpec(memory_space=pltpu.SMEM)
VMEM = pl.BlockSpec(memory_space=pltpu.VMEM)


def chunks(rows):
    return [(at, min(CHUNK, rows - at)) for at in range(0, rows, CHUNK)]


def run_all(copies):
    for copy in copies:
        copy.start()
    for copy in copies:
        copy.wait()


def arrange(scal, store, rate, mine, other, rate_m, sems):
    core, odd = scal[0], scal[1]
    rows = mine.shape[2]
    shift = rate.shape[1] // 2 - EDGE
    first = pl.multiple_of(core * shift, 8)
    second = pl.multiple_of((1 - core) * shift, 8)
    copies = []
    for m in range(4):
        layer = jnp.where(odd == 1, 3 - m, m)
        for start, target in ((second, other), (first, mine)):
            copies.append((store.at[0, :, layer, pl.ds(start, rows)], target.at[:, m]))
        copies.append((rate.at[layer, pl.ds(first, rows)], rate_m.at[pl.ds(rows * m, rows)]))
    run_all([pltpu.make_async_copy(a, b, sems.at[i]) for i, (a, b) in enumerate(copies)])


def parts(value):
    first = value.astype(jnp.bfloat16)
    rest = value - first.astype(jnp.float32)
    second = rest.astype(jnp.bfloat16)
    return [first, second, (rest - second.astype(jnp.float32)).astype(jnp.bfloat16)]


def exact_dot(a, b):
    return jnp.dot(a, b, precision=lax.Precision.HIGHEST, preferred_element_type=jnp.float32)


def window(scal, own, sib, out):
    half = own.shape[2] // 2
    for core in range(2):

        @pl.when(scal[0] == core)
        def _():
            at = core * (half - 1)
            for d in range(4):
                for k in range(2):
                    block = (own if d < 2 else sib)[d % 2, k, at : at + half + 1]
                    out[pl.ds((2 * d + k) * (half + 1), half + 1)] = block


def expand(scal, where, *refs):
    held, vfine, blocks = refs[:-2], refs[-2], refs[-1]
    core = scal[0]
    rows = vfine.shape[2]
    shift = rows - 2 * EDGE
    count = held[0].shape[1] // 8
    tall = blocks.shape[1]
    padded = (rows + 15) // 16 * 16
    row = lax.broadcasted_iota(jnp.int32, (padded, 4 * tall), 0) + core * shift
    column = lax.broadcasted_iota(jnp.int32, (padded, 4 * tall), 1)
    place = column % tall
    there = 4 * (place + core * (count - 2)) + column // tall
    pick_rows = ((row // 4 == there) & (place < count)).astype(jnp.float32)
    pick_rows = jnp.concatenate([pick_rows] * 3, 1).astype(jnp.bfloat16)
    lane = lax.broadcasted_iota(jnp.int32, (128, 512), 0)
    z = lax.broadcasted_iota(jnp.int32, (128, 512), 1)
    pick_lanes = (lane == 32 * (z // 128) + (z % 128) // 4).astype(jnp.float32)
    pick_lanes = jnp.concatenate([pick_lanes] * 3, 0).astype(jnp.bfloat16)
    blocks[...] = jnp.zeros(blocks.shape, jnp.float32)
    for k in range(8):
        for d in range(4):
            block = jnp.zeros((count, 128), jnp.float32)
            for i, ref in enumerate(held):
                for j in range(2):
                    for h in range(2):
                        hit = (where[k] == 2 * i + j) & (where[8 + k] == h)
                        block = jnp.where(hit, ref[j, pl.ds((2 * d + h) * count, count)], block)
            blocks[d, pl.ds(0, count)] = block
        wide = jnp.dot(
            jnp.concatenate(parts(blocks[...].reshape(4 * tall, 128)), 1),
            pick_lanes,
            preferred_element_type=jnp.float32,
        )
        table = jnp.concatenate(
            [
                jnp.concatenate(
                    [wide[tall * d : tall * (d + 1), 128 * j : 128 * (j + 1)] for j in range(4)], 0
                )
                for d in range(4)
            ],
            1,
        )
        filled = jnp.dot(
            pick_rows, jnp.concatenate(parts(table), 0), preferred_element_type=jnp.float32
        )[:rows]
        for d in range(4):
            vfine[d, k] = filled[:, 128 * d : 128 * (d + 1)]


def masks(rows):
    lane = lax.broadcasted_iota(jnp.int32, (rows, 128), 1)
    return lane == 0, lane == 127


def around(ref, lead, layer, before, after, at, rows):
    first, last = masks(rows)
    here = ref[lead, layer, pl.ds(PAD + at, rows)]
    total = ref[lead, layer, pl.ds(PAD - 1 + at, rows)] + ref[lead, layer, pl.ds(PAD + 1 + at, rows)]
    total = total + jnp.where(first, 0.0, pltpu.roll(here, 1, 1))
    total = total + jnp.where(last, 0.0, pltpu.roll(here, 127, 1))
    total = total + ref[lead, after, pl.ds(PAD + at, rows)]
    return here, total, ref[lead, before, pl.ds(PAD + at, rows)]


def clear_pads(ref, layers=None):
    dirs, every, rows, lanes = ref.shape
    zero = jnp.zeros((dirs, PAD, lanes), jnp.float32)

    @pl.loop(0, layers or every)
    def _(i):
        ref[:, i, pl.ds(0, PAD)] = zero
        ref[:, i, pl.ds(rows - PAD, PAD)] = zero


def clear_layer(ref, layer):
    ref[:, layer] = jnp.zeros((ref.shape[0], ref.shape[2], ref.shape[3]), jnp.float32)


def update(source, target, field_at, state_at, out_at, sigma, fields, weight, rows):
    p_ref, q_ref = source
    p_out, q_out, pad = target
    for at, n in chunks(rows):
        a = fields[0, field_at, pl.ds(at, n)]
        b = fields[1, field_at, pl.ds(at, n)]
        hold_a = keep_a - b
        hold_b = keep_b + a
        for d in range(4):
            p, p_sum, p_back = around(p_ref, d, state_at, state_at - sigma, state_at + sigma, at, n)
            q, q_sum, q_back = around(q_ref, d, state_at, state_at - sigma, state_at + sigma, at, n)
            w = weight[d, field_at, pl.ds(at, n)]
            p_out[d, out_at, pl.ds(pad + at, n)] = (
                spread_a * (p_sum + back_a * p_back) + hold_a * p - (a * q + w)
            )
            q_out[d, out_at, pl.ds(pad + at, n)] = (
                spread_b * (q_sum + back_b * q_back) + hold_b * q + (b * p + w)
            )


def weigh(low, high, rate, slab, v, q1):
    rows = rate.shape[1]

    @pl.loop(low, high)
    def _(i):
        coarse = (i + 2) // 2
        for at, n in chunks(rows):
            scaled = rate_scale * rate[i, pl.ds(at, n)]
            b = slab[1, i, pl.ds(at, n)]
            a = scaled * slab[0, i, pl.ds(at, n)]
            w = a * b
            slab[0, i, pl.ds(at, n)] = a
            slab[1, i, pl.ds(at, n)] = scaled * b
            for d in range(4):
                q1[d, i + 1, pl.ds(PAD + at, n)] = w * v[d, coarse, pl.ds(at, n)]


def outermost(far, layer, coarse, v, q1):
    for at, n in chunks(far.shape[0]):
        w = far[pl.ds(at, n)]
        for d in range(4):
            q1[d, layer, pl.ds(PAD + at, n)] = w * v[d, coarse, pl.ds(at, n)]


def second_update(low, high, sigma, slab, q1, p2, q2):
    rows = slab.shape[2]

    @pl.loop(low, high)
    def _(i):
        for at, n in chunks(rows):
            both = slab[0, i, pl.ds(at, n)] - slab[1, i, pl.ds(at, n)]
            hold_a = both + (1.0 + keep_a)
            hold_b = both + (1.0 + keep_b)
            for d in range(4):
                q, total, back = around(q1, d, i + 1, i + 1 - sigma, i + 1 + sigma, at, n)
                p2[d, i, pl.ds(PAD + at, n)] = -(spread_a * (total + back_a * back) + hold_a * q)
                q2[d, i, pl.ds(PAD + at, n)] = spread_b * (total + back_b * back) + hold_b * q


def third_update(low, high, sigma, slab, q1, p2, q2, p3, q3, shift):
    rows = slab.shape[2]

    @pl.loop(low, high)
    def _(i):
        for at, n in chunks(rows):
            a = slab[0, i + 1, pl.ds(at, n)]
            b = slab[1, i + 1, pl.ds(at, n)]
            hold_a = keep_a - b
            hold_b = keep_b + a
            for d in range(4):
                p, p_sum, p_back = around(p2, d, i + 1, i + 1 - sigma, i + 1 + sigma, at, n)
                q, q_sum, q_back = around(q2, d, i + 1, i + 1 - sigma, i + 1 + sigma, at, n)
                w = q1[d, i + 2, pl.ds(PAD + at, n)]
                p3[d, i - shift, pl.ds(PAD + at, n)] = (
                    spread_a * (p_sum + back_a * p_back) + hold_a * p - (a * q + w)
                )
                q3[d, i - shift, pl.ds(PAD + at, n)] = (
                    spread_b * (q_sum + back_b * q_back) + hold_b * q + (b * p + w)
                )


def first_step(
    scal, rate_m, rate_e, rate_l, s_a, s_b, e_a, e_b, l_a, far_e, v,
    state, edge1, edge2, edge_slab, rate, slab, far, q1, p2, q2, sems,
):
    sigma = 1 - 2 * scal[1]
    has_late = scal[2]
    p3, q3 = state.at[0], state.at[1]
    rows = rate.shape[1]
    moves = [(rate_m.at[pl.ds(rows * j, rows)], rate.at[4 + j]) for j in range(4)]
    moves += [(s_a, slab.at[:, pl.ds(4, 2)]), (s_b, slab.at[:, pl.ds(6, 2)])]
    for j in range(4):
        moves.append((rate_e.at[pl.ds(rows * j, rows)], rate.at[11 - j]))
    for j in range(2):
        moves.append((rate_l.at[pl.ds(rows * j, rows)], rate.at[3 - j]))
        moves.append((e_a.at[:, j], slab.at[:, 11 - j]))
        moves.append((e_b.at[:, j], slab.at[:, 9 - j]))
        moves.append((l_a.at[:, j], slab.at[:, 3 - j]))
    moves.append((far_e, far))
    copies = [pltpu.make_async_copy(a, b, sems.at[i]) for i, (a, b) in enumerate(moves)]
    for copy in copies:
        copy.start()
    for ref in (q1, p2, q2, p3, q3):
        clear_pads(ref)

    @pl.when(has_late == 0)
    def _():
        for ref in (p2, q2):
            clear_layer(ref, 3)

    for copy in copies:
        copy.wait()
    outermost(far, 13, 7, v, q1)
    weigh(2, 12, rate, slab, v, q1)
    second_update(jnp.where(has_late == 1, 3, 4), 12, sigma, slab, q1, p2, q2)
    moves = [(q1.at[:, pl.ds(3, 2)], edge1), (slab.at[:, pl.ds(2, 2)], edge_slab)]
    moves += [(p2.at[:, pl.ds(3, 2)], edge2.at[0]), (q2.at[:, pl.ds(3, 2)], edge2.at[1])]
    copies = [pltpu.make_async_copy(a, b, sems.at[i]) for i, (a, b) in enumerate(moves)]
    for copy in copies:
        copy.start()
    third_update(3, 10, sigma, slab, q1, p2, q2, p3, q3, 3)
    for copy in copies:
        copy.wait()


def late_layers(
    scal, rate_l, l_b, far_l, v, state, edge1, edge2, edge_slab,
    late, rate, slab, far, q1, p2, q2, sems,
):
    sigma = 1 - 2 * scal[1]
    rows = rate.shape[1]
    p3, q3 = late.at[0], late.at[1]
    kept = [
        pltpu.make_async_copy(state.at[i, :, pl.ds(0, 2)], late.at[i, :, pl.ds(3, 2)], sems.at[i])
        for i in range(2)
    ]
    for copy in kept:
        copy.start()

    @pl.when(scal[2] == 0)
    def _():
        for ref in (p3, q3):
            clear_layer(ref, 2)

    @pl.when(scal[2] == 1)
    def _():
        moves = [(far_l, far), (edge1, q1.at[:, pl.ds(3, 2)]), (edge_slab, slab.at[:, pl.ds(2, 2)])]
        moves += [(edge2.at[0], p2.at[:, pl.ds(3, 2)]), (edge2.at[1], q2.at[:, pl.ds(3, 2)])]
        for j in range(2):
            moves.append((rate_l.at[pl.ds(rows * (2 + j), rows)], rate.at[1 - j]))
            moves.append((l_b.at[:, j], slab.at[:, 1 - j]))
        copies = [pltpu.make_async_copy(a, b, sems.at[2 + i]) for i, (a, b) in enumerate(moves)]
        for copy in copies:
            copy.start()
        for ref in (q1, p2, q2, p3, q3):
            clear_pads(ref, 3)
        for copy in copies:
            copy.wait()
        outermost(far, 0, 0, v, q1)
        weigh(0, 2, rate, slab, v, q1)
        second_update(0, 3, sigma, slab, q1, p2, q2)
        third_update(0, 3, sigma, slab, q1, p2, q2, p3, q3, 0)

    for copy in kept:
        copy.wait()


def second_step(
    scal, rate_m, rate_e, rate_l, s_a, s_b, e_b, l_a, v, state, late,
    tangent, sent, means, means_sib, rate, slab, weight, p4, q4, p5, q5, p6, q6, sems, out_sems,
):
    core, odd, has_late = scal[0], scal[1], scal[2]
    sigma = 1 - 2 * odd
    rows = rate.shape[1]
    half = rows - EDGE
    moves = [(rate_m.at[pl.ds(rows * j, rows)], rate.at[2 + j]) for j in range(4)]
    moves += [(s_a, slab.at[:, pl.ds(2, 2)]), (s_b, slab.at[:, pl.ds(4, 2)])]
    for j in range(2):
        moves.append((rate_e.at[pl.ds(rows * (3 - j), rows)], rate.at[6 + j]))
        moves.append((rate_l.at[pl.ds(rows * j, rows)], rate.at[1 - j]))
        moves.append((e_b.at[:, 1 - j], slab.at[:, 6 + j]))
        moves.append((l_a.at[:, j], slab.at[:, 1 - j]))
    copies = [pltpu.make_async_copy(a, b, sems.at[i]) for i, (a, b) in enumerate(moves)]
    for copy in copies:
        copy.start()
    for ref in (p4, q4, p5, q5):
        clear_pads(ref)

    @pl.when(has_late == 0)
    def _():
        for ref, layer in ((p4, 1), (q4, 1), (p5, 0), (q5, 0)):
            clear_layer(ref, layer)

    for copy in copies:
        copy.wait()

    @pl.loop(0, 8)
    def _(i):
        coarse = i // 2 + 2
        for at, n in chunks(rows):
            scaled = rate_scale * rate[i, pl.ds(at, n)]
            b = slab[1, i, pl.ds(at, n)]
            a = scaled * slab[0, i, pl.ds(at, n)]
            w = a * b
            slab[0, i, pl.ds(at, n)] = a
            slab[1, i, pl.ds(at, n)] = scaled * b
            for d in range(4):
                weight[d, i, pl.ds(at, n)] = w * v[d, coarse, pl.ds(at, n)]

    @pl.loop(jnp.where(has_late == 1, 0, 2), 3)
    def _(i):
        update((late.at[0], late.at[1]), (p4, q4, PAD), i, i + 1, i, sigma, slab, weight, rows)

    @pl.loop(3, 8)
    def _(i):
        update((state.at[0], state.at[1]), (p4, q4, PAD), i, i - 2, i, sigma, slab, weight, rows)

    @pl.loop(jnp.where(has_late == 1, 0, 1), 6)
    def _(i):
        update((p4, q4), (p5, q5, PAD), i + 1, i + 1, i, sigma, slab, weight, rows)

    start = pl.multiple_of(core * EDGE, 8)
    place = pl.multiple_of(core * half, 8)

    def writes(i):
        layer = jnp.where(odd == 1, 3 - i, i)
        for j, ref in enumerate((p6, q6)):
            yield pltpu.make_async_copy(
                ref.at[pl.ds(0, 2), i, pl.ds(start, half)],
                tangent.at[:, j, layer, pl.ds(place, half)],
                out_sems.at[i, j],
            )
            yield pltpu.make_async_copy(
                ref.at[pl.ds(2, 2), i, pl.ds(start, half)],
                sent.at[:, j, layer],
                out_sems.at[i, 2 + j],
            )

    @pl.loop(0, 4)
    def _(i):
        update((p5, q5), (p6, q6, 0), i + 2, i + 1, i, sigma, slab, weight, rows)
        for copy in writes(i):
            copy.start()

    packed = half // 16
    row = lax.broadcasted_iota(jnp.int32, (4 * packed, half), 0)
    column = lax.broadcasted_iota(jnp.int32, (4 * packed, half), 1)
    sum_rows = (column // 4 == 4 * (row % packed) + row // packed).astype(jnp.float32)
    lane = lax.broadcasted_iota(jnp.int32, (512, 128), 1)
    z = lax.broadcasted_iota(jnp.int32, (512, 128), 0)
    sum_lanes = (lane == 32 * (z // 128) + (z % 128) // 4).astype(jnp.float32)
    pairs = [
        q6[d, 2 * k, pl.ds(start, half)] + q6[d, 2 * k + 1, pl.ds(start, half)]
        for d in range(4)
        for k in range(2)
    ]
    summed = exact_dot(sum_rows, jnp.concatenate(pairs, 1))
    spread = jnp.concatenate(
        [
            jnp.concatenate(
                [summed[packed * j : packed * (j + 1), 128 * i : 128 * (i + 1)] for j in range(4)], 1
            )
            for i in range(8)
        ],
        0,
    )
    total = exact_dot(spread, sum_lanes) * (1.0 / 32.0)
    for d in range(4):
        for k in range(2):
            layer = jnp.where(odd == 1, 1 - k, k)
            (means if d < 2 else means_sib)[d % 2, layer] = total[packed * (2 * d + k) : packed * (2 * d + k + 1)]

    @pl.loop(0, 4)
    def _(i):
        for copy in writes(i):
            copy.wait()


def finish(scal, held, received, tangent, sems):
    half = received.shape[3]
    place = pl.multiple_of((1 - scal[0]) * half, 8)
    run_all(
        [
            pltpu.make_async_copy(
                received.at[i, j], tangent.at[i, j, :, pl.ds(place, half)], sems.at[i, j]
            )
            for i in range(2)
            for j in range(2)
        ]
    )


def cost(flops, moved):
    return pl.CostEstimate(flops=flops, bytes_accessed=moved, transcendentals=0)


def after(value, *others):
    return lax.optimization_barrier((value, *others))[0]


def params(megabytes):
    return pltpu.CompilerParams(vmem_limit_bytes=megabytes << 20)


def stay(value):
    return pltpu.with_memory_space_constraint(value, pltpu.VMEM)


def vmem(*dims):
    return pltpu.VMEM(dims, jnp.float32)


def shape(*dims):
    return jax.ShapeDtypeStruct(dims, jnp.float32)


def local(store, rate, directions, owner_map, block_map):
    layers, width_y, width_z = rate.shape
    half = width_y // 2
    rows = half + EDGE
    n_space = lax.axis_size("space")
    mine = lax.axis_index("space")
    group = lax.axis_index("dir")
    core, column = group & 1, group >> 1
    odd = mine & 1
    has_late = ((mine > 0) & (mine < n_space - 1)).astype(jnp.int32)
    scal = jnp.stack([core, odd, has_late]).astype(jnp.int32)

    across_core = [(i, i ^ 1) for i in range(4)]
    across_column = [(i, i ^ 2) for i in range(4)]
    swap = [(i, i ^ 1) for i in range(n_space)]
    ahead = [(i, i + 2) for i in range(0, n_space - 2, 2)] + [(i, i - 2) for i in range(3, n_space, 2)]
    behind = [(b, a) for a, b in ahead]
    to_core = functools.partial(lax.ppermute, axis_name="dir", perm=across_core)
    to_column = functools.partial(lax.ppermute, axis_name="dir", perm=across_column)
    to_pair = functools.partial(lax.ppermute, axis_name="space", perm=swap)
    to_ahead = functools.partial(lax.ppermute, axis_name="space", perm=ahead)
    to_behind = functools.partial(lax.ppermute, axis_name="space", perm=behind)

    row = directions.reshape(2, 2, 32, 128)
    with jax.named_scope("directions_core"):
        row_sib = to_core(row)
    own, other, rate_m = pl.pallas_call(
        arrange,
        out_shape=(vmem(2, 4, rows, width_z), vmem(2, 4, rows, width_z), vmem(4 * rows, width_z)),
        in_specs=[SMEM, ANY, ANY],
        out_specs=[VMEM] * 3,
        cost_estimate=cost(0, 6 << 20),
        scratch_shapes=[pltpu.SemaphoreType.DMA((12,))],
        name="arrange",
    )(scal, store, rate)
    with jax.named_scope("store_core"):
        received = to_core(other)

    def candidates(step, received):
        here = group == owner_map[step]
        first = jnp.where(here, own[:, :2], received[:, :2])
        return first, jnp.where(here, own[:, 2:], after(received, first)[:, 2:])

    def settled(step, have, came):
        return jnp.where(column == owner_map[step] >> 1, have, came)

    have0_a, have0_b = candidates(0, received)
    have1_a, have1_b = candidates(1, after(received, have0_a))

    coarse_own = pl.pallas_call(
        window,
        out_shape=vmem(8 * 17, 128),
        in_specs=[SMEM, VMEM, VMEM],
        out_specs=VMEM,
        name="window",
    )(scal, after(row, rate_m), row_sib)
    with jax.named_scope("directions_pair"):
        pair = jnp.stack([coarse_own, after(to_pair(coarse_own), have0_b)])
    held = [pair]
    for j in range(2, n_space, 2):
        with jax.named_scope("directions_space"):
            held.append(lax.ppermute(after(pair), "space", [(i, i ^ j) for i in range(n_space)]))
    with jax.named_scope("rate_pair"):
        rate_e = to_pair(after(rate_m, received))
    with jax.named_scope("slab0_column"):
        came0_a = to_column(after(have0_a))
        came0_b = to_column(after(have0_b, came0_a, have1_a, have1_b))
    with jax.named_scope("rate_ahead"):
        rate_l = to_ahead(after(rate_e))
    s0_a = settled(0, have0_a, came0_a)
    with jax.named_scope("slab0_pair"):
        e0_a = to_pair(after(s0_a, rate_e, *held))
    s0_b = settled(0, have0_b, after(came0_b))
    w_near = rate_scale * rate_m[:rows] * s0_a[0, 0] * s0_a[1, 0]
    w_late = rate_scale * rate_m[3 * rows : 4 * rows] * s0_b[0, 1] * s0_b[1, 1]
    with jax.named_scope("far_layers"):
        far_e = to_behind(after(w_near, rate_l))
        far_l = to_ahead(after(w_late, rate_l))
    with jax.named_scope("slab1_column"):
        came1_a = to_column(after(have1_a, e0_a))
    local_coarse = jnp.arange(8, dtype=jnp.int32) - 3
    coarse_at = 2 * mine + jnp.where(odd == 1, 1 - local_coarse, local_coarse)
    block = block_map[jnp.clip(coarse_at >> 1, 0, n_space - 1)] ^ mine
    coarse_scal = jnp.concatenate([block, coarse_at & 1]).astype(jnp.int32)
    vfine = pl.pallas_call(
        expand,
        out_shape=vmem(4, 8, rows, width_z),
        in_specs=[SMEM, SMEM] + [VMEM] * len(held),
        out_specs=VMEM,
        scratch_shapes=[vmem(4, 24, 128)],
        name="expand",
        cost_estimate=cost(0, 25 << 20),
        compiler_params=params(16),
    )(scal, coarse_scal, *held[:-1], after(held[-1]))
    with jax.named_scope("slab0_pair"):
        e0_b = to_pair(after(s0_b, e0_a))
    with jax.named_scope("slab1_column"):
        came1_b = to_column(after(have1_b, e0_b, far_e, far_l))
    with jax.named_scope("slab0_ahead"):
        l0_a = to_ahead(after(e0_a, s0_b))
        l0_b = to_ahead(after(e0_b, l0_a, far_e, far_l, vfine))
    s1_a = settled(1, have1_a, came1_a)
    with jax.named_scope("slab1_pair"):
        e1_a = to_pair(after(s1_a, e0_b))
    with jax.named_scope("slab1_ahead"):
        l1_a = to_ahead(after(e1_a, l0_b))
    tall = rows + 2 * PAD
    state, *edges = pl.pallas_call(
        first_step,
        out_shape=(
            vmem(2, 4, 7, tall, width_z),
            vmem(4, 2, tall, width_z),
            vmem(2, 4, 2, tall, width_z),
            vmem(2, 2, rows, width_z),
        ),
        in_specs=[SMEM] + [ANY] * 9 + [VMEM],
        out_specs=[VMEM] * 4,
        scratch_shapes=[
            vmem(12, rows, width_z),
            vmem(2, 12, rows, width_z),
            vmem(rows, width_z),
            vmem(4, 14, tall, width_z),
            vmem(4, 12, tall, width_z),
            vmem(4, 12, tall, width_z),
            pltpu.SemaphoreType.DMA((19,)),
        ],
        name="first_step",
        cost_estimate=cost(0, 40 << 20),
        compiler_params=params(30),
    )(scal, rate_m, rate_e, rate_l, s0_a, s0_b, e0_a, e0_b, after(l0_a), far_e, stay(vfine))
    s1_b = settled(1, have1_b, after(came1_b, state))
    with jax.named_scope("slab1_pair"):
        e1_b = to_pair(after(s1_b))

    l0_b = after(l0_b, e1_a, s1_b)

    late = pl.pallas_call(
        late_layers,
        out_shape=vmem(2, 4, 5, tall, width_z),
        in_specs=[SMEM] + [ANY] * 3 + [VMEM] * 5,
        out_specs=VMEM,
        scratch_shapes=[
            vmem(2, rows, width_z),
            vmem(2, 4, rows, width_z),
            vmem(rows, width_z),
            vmem(4, 5, tall, width_z),
            vmem(4, 5, tall, width_z),
            vmem(4, 5, tall, width_z),
            pltpu.SemaphoreType.DMA((11,)),
        ],
        name="late_layers",
        cost_estimate=cost(0, 20 << 20),
        compiler_params=params(12),
    )(scal, rate_l, l0_b, far_l, stay(vfine), stay(state), *[stay(x) for x in edges])

    tangent, sent, first, second = pl.pallas_call(
        second_step,
        out_shape=(
            shape(2, 2, 4, width_y, width_z),
            shape(2, 2, 4, half, width_z),
            vmem(2, 2, half // 16, 128),
            vmem(2, 2, half // 16, 128),
        ),
        in_specs=[SMEM] + [ANY] * 7 + [VMEM] * 3,
        out_specs=[ANY, ANY, VMEM, VMEM],
        scratch_shapes=[
            vmem(8, rows, width_z),
            vmem(2, 8, rows, width_z),
            vmem(4, 8, rows, width_z),
            vmem(4, 8, tall, width_z),
            vmem(4, 8, tall, width_z),
            vmem(4, 6, tall, width_z),
            vmem(4, 6, tall, width_z),
            vmem(4, 4, rows, width_z),
            vmem(4, 4, rows, width_z),
            pltpu.SemaphoreType.DMA((14,)),
            pltpu.SemaphoreType.DMA((4, 4)),
        ],
        name="second_step",
        cost_estimate=cost(0, 55 << 20),
        compiler_params=params(36),
    )(scal, rate_m, rate_e, rate_l, s1_a, s1_b, e1_b, l1_a, stay(vfine), stay(state), stay(late))


    def joined(a, b):
        return jnp.where(core == 0, jnp.concatenate([a, b], 2), jnp.concatenate([b, a], 2))

    both = [(i * n_space + j, (i ^ 1) * n_space + (j ^ 1)) for i in range(4) for j in range(n_space)]
    with jax.named_scope("means_near"):
        here = joined(first, to_core(second))
        there = joined(to_pair(first), lax.ppermute(second, ("dir", "space"), both))
    with jax.named_scope("tangent_core"):
        rest = to_core(sent)
    source = jnp.sum(jnp.where(block_map == mine, jnp.arange(n_space, dtype=jnp.int32), 0))
    sens = jnp.where(source == mine, here, there)
    came = []
    for j in range(2, n_space, 2):
        row = after(jnp.where(block_map[mine] == mine ^ j, here, there), rest)
        pairs = [(i, i ^ j) for i in range(n_space)]
        with jax.named_scope("means_space"):
            came.append(lax.ppermute(row, "space", pairs))
    tangent = pl.pallas_call(
        finish,
        out_shape=shape(2, 2, 4, width_y, width_z),
        in_specs=[SMEM, ANY, VMEM],
        out_specs=ANY,
        scratch_shapes=[pltpu.SemaphoreType.DMA((2, 2))],
        input_output_aliases={1: 0},
        cost_estimate=cost(0, 2 << 22),
        name="finish",
    )(scal, tangent, rest)
    came[0] = after(came[0], tangent)
    for j, row in zip(range(2, n_space, 2), came):
        sens = jnp.where(source >> 1 == (mine ^ j) >> 1, row, sens)
    return tangent, sens.reshape(2, 1, -1)


def solution(mesh):
    return jax.shard_map(
        local,
        mesh=mesh,
        in_specs=(
            P("dir", None, "space", None, None),
            P("space", None, None),
            P("dir", "space", None),
            P(),
            P(),
        ),
        out_specs=(P("dir", None, "space", None, None), P("dir", "space", None)),
        check_vma=False,
    )
```
